32 devices in a mesh: grp: 2 (over y), lat: 4 (over z), lon: 2 (over x), role: 2 (over core).
Axes of the slice: x: 2, y: 2, z: 4, core: 2. Of those that a mesh axis runs over, the one named last changes fastest.
Arguments:
- eastern_edge_current: float32 [8, 128, 256], P('lon', ('grp', 'lat', 'role')), parts along dimension 1, may hold values from -1.5 to 1.5
- northern_edge_current: float32 [8, 128, 256], P('lon', ('grp', 'lat', 'role')), parts along dimension 1, may hold values from -1.5 to 1.5
- thermal_anomaly: float32 [8, 128, 256], P('lon', ('grp', 'lat', 'role')), parts along dimension 1, may hold values from -6 to 6
- prior_warming: float32 [8, 128, 256], P('lon', ('grp', 'lat', 'role')), parts along dimension 1, may hold values from 0 to 0.5
- solute_fields: float32 [24, 8, 128, 256], P(None, None, ('grp', 'lat', 'role'), 'lon'), parts along dimension 2, may hold values from -6 to 6
- submerged_layer_count: int32 [128, 256], P(('grp', 'lat', 'role')), parts along dimension 0, may hold values from 0 to 8
- reaction_rates: float32 [24, 24], replicated, may hold values from -1.25 to 1.25
Outputs:
- u_out: float32 [8, 128, 256], P('lon', ('grp', 'lat', 'role')), parts along dimension 1
- v_out: float32 [8, 128, 256], P('lon', ('grp', 'lat', 'role')), parts along dimension 1
- temp_out: float32 [8, 128, 256], P('lon', ('grp', 'lat', 'role')), parts along dimension 1
- heating_out: float32 [8, 128, 256], P('lon', ('grp', 'lat', 'role')), parts along dimension 1
- tracers_out: float32 [24, 8, 128, 256], P(None, None, ('grp', 'lat', 'role'), 'lon'), parts along dimension 2
The draws below stay inside these ranges and needn't reach their ends.
There are 2 independent parts, one for each index of `grp`. The reference program is written for one: setup_inputs(seed, part) draws one part's arguments, and reference() takes and returns one part's arrays. A program takes and returns all parts, laid end to end along the dimension named above; an argument that names none is the same for every part. Nothing has to cross between parts.
All inputs are finite; a program needn't handle non-finite values.
Results may differ from the reference program's by a relative error of at most 0.0001.
Values sent between devices are 32-bit elements; how exact they have to be, the bound alone decides.
No kernel may reach another device: no remote copies, remote signals or barrier semaphores. Data moves between devices by JAX's collectives and lax.ppermute only.
A program may use at most 64 MiB of HBM per device.

```python
import jax
import jax.numpy as jnp
from jax import lax

TR = 24
DEPTH_LAYERS = 8
STEPS = 2
GRID_PARALLELS = 64
GRID_MERIDIANS = 256


def place_ends(array, key, low, high):
    longest = array.shape.index(max(array.shape))
    spots = []
    for shift in (0, 1):
        where = [jax.random.randint(jax.random.fold_in(key, axis), (), 0, length) for axis, length in enumerate(array.shape)]
        where[longest] = (where[longest] + shift) % array.shape[longest]
        spots.append(tuple(where))
    return array.at[spots[0]].set(low).at[spots[1]].set(high)


def shard_levels(key, shape, shards, low, high):
    level, own = 1.0, jax.random.fold_in(key, 6)
    for position, parts in shards:
        steps = jnp.exp(jax.random.uniform(jax.random.fold_in(own, position), (parts,), jnp.float32, low / len(shards), high / len(shards)))
        level = level * jnp.repeat(steps, shape[position] // parts).reshape([-1 if axis == position else 1 for axis in range(len(shape))])
    return level


def scatter_about(rng, extent, spread, limit, split=(), kind=jnp.bfloat16):
    values = jax.random.normal(rng, extent, jnp.float32) * spread
    if len(split) > 0:
        values = shard_levels(rng, extent, split, -0.22, 0.18) * values
    return jnp.clip(values, min=-limit, max=limit).astype(kind)


def setup_inputs(seed: int = 0, part: int = 0) -> dict:
    key_list = jax.random.split(jax.random.key(seed), 8)
    part_keys = jax.random.split(jax.random.fold_in(key_list[7], part), 8)
    return {
        "eastern_edge_current": scatter_about(part_keys[0], (DEPTH_LAYERS, GRID_PARALLELS, GRID_MERIDIANS), 0.3, 1.5, ((0, 2), (1, 8)), jnp.float32),
        "northern_edge_current": scatter_about(part_keys[1], (DEPTH_LAYERS, GRID_PARALLELS, GRID_MERIDIANS), 0.3, 1.5, ((0, 2), (1, 8)), jnp.float32),
        "thermal_anomaly": scatter_about(part_keys[2], (DEPTH_LAYERS, GRID_PARALLELS, GRID_MERIDIANS), 1.0, 6.0, ((0, 2), (1, 8)), jnp.float32),
        "prior_warming": jnp.clip(0.5 * jax.random.uniform(part_keys[3], (DEPTH_LAYERS, GRID_PARALLELS, GRID_MERIDIANS), jnp.float32) ** shard_levels(part_keys[3], (DEPTH_LAYERS, GRID_PARALLELS, GRID_MERIDIANS), ((0, 2), (1, 8)), -0.2, 0.2), 0.0, 0.5),
        "solute_fields": scatter_about(part_keys[4], (TR, DEPTH_LAYERS, GRID_PARALLELS, GRID_MERIDIANS), 1.0, 6.0, ((2, 8), (3, 2)), jnp.float32),
        "submerged_layer_count": place_ends(jax.random.randint(part_keys[5], (GRID_PARALLELS, GRID_MERIDIANS), 0, DEPTH_LAYERS + 1), jax.random.fold_in(part_keys[5], 1), 0, DEPTH_LAYERS).astype(jnp.int32),
        "reaction_rates": scatter_about(key_list[6], (TR, TR), TR ** -0.5, 1.25, (), jnp.float32),
    }


def eastern_neighbor(q):
    return jnp.concatenate([q[..., 1:], jnp.zeros_like(q[..., :1])], axis=-1)


def west(q):
    return jnp.concatenate([jnp.zeros_like(q[..., :1]), q[..., :-1]], axis=-1)


def northern_neighbor(q):
    return jnp.concatenate([q[..., 1:, :], jnp.zeros_like(q[..., :1, :])], axis=-2)


def south(q):
    return jnp.concatenate([jnp.zeros_like(q[..., :1, :]), q[..., :-1, :]], axis=-2)


def diffusion_operator(q):
    return eastern_neighbor(q) + west(q) + northern_neighbor(q) + south(q) - 4.0 * q


def reference(eastern_edge_current, northern_edge_current, thermal_anomaly, prior_warming, solute_fields, submerged_layer_count, reaction_rates):
    levels = jnp.arange(DEPTH_LAYERS, dtype=jnp.int32)
    ocean_mask = (levels[:, None, None] < submerged_layer_count[None, :, :]).astype(jnp.float32)
    ocean_mask_eastward = ocean_mask * eastern_neighbor(ocean_mask)
    ocean_mask_poleward = ocean_mask * northern_neighbor(ocean_mask)
    coriolis_parameter = (2.0 * (jnp.arange(GRID_PARALLELS, dtype=jnp.float32) + 0.5) / GRID_PARALLELS - 1.0)[:, None]
    thermal_energy = prior_warming
    eastward_current, poleward_current, seawater_warmth, solute_amount = eastern_edge_current, northern_edge_current, thermal_anomaly, solute_fields
    for step in range(STEPS):
        updated_eastward_flow = ocean_mask_eastward * (eastward_current + 0.1 * diffusion_operator(eastward_current) + 0.3 * coriolis_parameter * poleward_current - 0.2 * (eastern_neighbor(seawater_warmth) - seawater_warmth))
        updated_poleward_flow = ocean_mask_poleward * (poleward_current + 0.1 * diffusion_operator(poleward_current) - 0.3 * coriolis_parameter * eastward_current - 0.2 * (northern_neighbor(seawater_warmth) - seawater_warmth))
        seawater_warmth = ocean_mask * (seawater_warmth + 0.1 * diffusion_operator(seawater_warmth) + 0.5 * thermal_energy)
        eastward_current, poleward_current = updated_eastward_flow, updated_poleward_flow
        flux_x = jnp.maximum(eastward_current, 0.0) * solute_amount + jnp.minimum(eastward_current, 0.0) * eastern_neighbor(solute_amount)
        flux_y = jnp.maximum(poleward_current, 0.0) * solute_amount + jnp.minimum(poleward_current, 0.0) * northern_neighbor(solute_amount)
        advected = solute_amount - 0.5 * ((flux_x - west(flux_x)) + (flux_y - south(flux_y)))
        atten = 0.1 + 0.3 * jnp.maximum(advected[0], 0.0)
        summed = jnp.cumsum(atten, axis=0)
        depth_tau = jnp.concatenate([jnp.zeros_like(atten[:1]), summed[:-1]], axis=0)
        top = jnp.exp(-depth_tau)
        thermal_energy = 2.0 * ocean_mask * (top - jnp.exp(-(depth_tau + atten)))
        react = jnp.einsum("ab,bzyx->azyx", reaction_rates, advected, precision=lax.Precision.HIGHEST)
        solute_amount = ocean_mask * (advected + 0.5 * top * react)
    return eastward_current, poleward_current, seawater_warmth, thermal_energy, solute_amount
```

```python
import functools

import jax
import jax.numpy as jnp
from jax import lax
from jax.experimental import pallas as pl
from jax.experimental.pallas import tpu as pltpu
from jax.sharding import PartitionSpec as P

STEPS = 2
ROWS = 8
LANES = 128
LEVELS = 8
CORES = 2

FIELDS = 4
DYN = FIELDS * LEVELS
CHL = DYN
SUM = CHL + LEVELS
EDGE = SUM + LEVELS
X_TILES = EDGE + LEVELS
DYN2 = DYN // 2
MIX2 = DYN2 + LEVELS
XZ_TILES = MIX2 + 1


def iota(shape, dim):
    return lax.broadcasted_iota(jnp.int32, shape, dim)


def roll(q, shift, axis):
    return pltpu.roll(q, shift % q.shape[axis], axis)


def pack_kernel(n, pos, rates, u, v, t, h, count, c, x_out, z_out, r_out, xz_out):
    tracers = c.shape[0]
    share = u.shape[0]
    upper = pos[2] == 1
    sub = iota((ROWS, LANES), 0)
    lane = iota((ROWS, LANES), 1)
    to_z = (sub >= ROWS // 2) == upper

    def halves(a, b):
        moved = roll(b, ROWS // 2, 0)
        return jnp.where(to_z, a, moved), jnp.where(to_z, moved, a)

    fields = (u, v, t, h)
    for level in range(share):
        for block in range(n):
            cols = slice(block * LANES, (block + 1) * LANES)
            tiles = [f[level, :, cols] for f in fields]
            place = level * n + block
            for f in range(FIELDS):
                x_out[f * LEVELS + place] = tiles[f]
            for pair in range(2):
                forth, across = halves(tiles[2 * pair], tiles[2 * pair + 1])
                z_out[pair * LEVELS + place] = forth
                xz_out[pair * LEVELS + place] = forth
                r_out[pair * LEVELS + place] = across
    for block in range(n):
        depth = count[:, block * LANES : (block + 1) * LANES].astype(jnp.float32)
        z_out[DYN2 + block] = depth
        r_out[DYN2 + block] = depth

    def one_level(k, carry):
        total = jnp.zeros((ROWS, LANES), jnp.float32)
        edge = jnp.zeros((ROWS, LANES), jnp.float32)
        for b in range(tracers):
            q = c[b, k]
            total = total + rates[0, b] * q
            edge = jnp.where(lane // 4 == b, roll(q, 4 * b + 2, 1), edge)
        x_out[CHL + k] = c[0, k]
        x_out[SUM + k] = total
        x_out[EDGE + k] = edge
        forth, _ = halves(c[0, k], total)
        xz_out[DYN2 + k] = forth
        return carry

    lax.fori_loop(0, LEVELS, one_level, 0)
    edges = [x_out[EDGE : EDGE + LEVELS, row, :] for row in (0, ROWS - 1)]
    xz_out[MIX2] = jnp.where(upper, edges[1], edges[0])
    base = DYN2 + n
    for b in range(tracers + 1):
        for far in range(2):
            low, high = far, ROWS - 1 - far
            if b < tracers:
                bottom, top = c[b, :, low, :], c[b, :, high, :]
            else:
                bottom, top = x_out[SUM : SUM + LEVELS, low, :], x_out[SUM : SUM + LEVELS, high, :]
            z_out[base + 2 * b + far] = jnp.where(upper, top, bottom)
            r_out[base + 2 * b + far] = jnp.where(upper, bottom, top)


def split(q):
    high = q.astype(jnp.bfloat16)
    return high, (q - high.astype(jnp.float32)).astype(jnp.bfloat16)


def spread_kernel(rates, m_high, m_low, e_high, e_low):
    tracers = rates.shape[0]
    exact = functools.partial(jnp.dot, precision=lax.Precision.HIGHEST, preferred_element_type=jnp.float32)
    for group, transposed, high, low in ((ROWS, False, m_high, m_low), (4, True, e_high, e_low)):
        size = high.shape[0]
        rows = (iota((size, tracers), 0) // group == iota((size, tracers), 1)).astype(jnp.float32)
        cols = (iota((tracers, size), 1) // group == iota((tracers, size), 0)).astype(jnp.float32)
        wide = exact(exact(rows, rates[...].T if transposed else rates[...]), cols)
        same = iota((size, size), 0) % group == iota((size, size), 1) % group
        high[...], low[...] = split(jnp.where(same, wide, 0.0))


def exact_product(left, right):
    dot = functools.partial(jnp.dot, preferred_element_type=jnp.float32)
    return dot(left[0], right[0]) + (dot(left[0], right[1]) + dot(left[1], right[0]))


def step_kernel(n, strips, *refs):
    pos, u, v, t, h, count, c, own, m_high, m_low, e_high, e_low, z, r = refs[:14]
    others = n - 1
    xs, r2s, xzs = (refs[14 + i * others : 14 + (i + 1) * others] for i in range(3))
    u_out, v_out, t_out, h_out, c_out = refs[14 + 3 * others : 19 + 3 * others]
    dyn, mix, depth, coef, row0, row1, edge0, corner, edge1, adv, mid, out4 = refs[19 + 3 * others :]
    tracers = c.shape[0]
    share = u.shape[0]
    width = n * LANES
    strip, lon, role = pos[0], pos[1], pos[2]
    upper = role == 1
    base = DYN2 + n

    sub = iota((ROWS, LANES), 0)
    lane = iota((ROWS, LANES), 1)
    from_r = (sub >= ROWS // 2) == upper
    no_south, no_north = strip == 0, strip == strips - 1
    lost = jnp.logical_or(no_south, no_north)
    lost_z = jnp.logical_or(
        jnp.logical_and(no_south, jnp.logical_not(upper)), jnp.logical_and(no_north, upper)
    )
    keep_z = jnp.where(lost_z, 0.0, 1.0)
    del lost

    def halo(near, far):
        return jnp.where(from_r, near, jnp.where(lost_z, 0.0, far))

    def block_of(m):
        return pl.ds(pl.multiple_of(m * LANES, LANES), LANES)

    fields = (u, v, t, h)
    for level in range(share):
        for block in range(n):
            cols = slice(block * LANES, (block + 1) * LANES)
            place = level * n + block
            for pair in range(2):
                near, far = r[pair * LEVELS + place], z[pair * LEVELS + place]
                for second in range(2):
                    f = 2 * pair + second
                    if second:
                        near, far = roll(near, ROWS // 2, 0), roll(far, ROWS // 2, 0)
                    dyn[f, lon * share + level, :ROWS, cols] = fields[f][level, :, cols]
                    dyn[f, lon * share + level, ROWS:, cols] = halo(near, far)
    for block in range(n):
        cols = slice(block * LANES, (block + 1) * LANES)
        depth[:ROWS, cols] = count[:, cols].astype(jnp.float32)
        depth[ROWS:, cols] = halo(r[DYN2 + block], z[DYN2 + block])

    def near_rows(b, far):
        a, d = r[base + 2 * b + far], z[base + 2 * b + far] * keep_z
        return jnp.where(upper, a, d), jnp.where(upper, d, a)

    here = block_of(lon)
    mix[0, :, :ROWS, here] = c[0]
    mix[1, :, :ROWS, here] = own[SUM : SUM + LEVELS]
    for i, b in enumerate((0, tracers)):
        for far in range(2):
            south, north = near_rows(b, far)
            mix[i, :, ROWS + far, here] = north
            mix[i, :, 2 * ROWS - 1 - far, here] = south

    for s, (x, r2, xz) in enumerate(zip(xs, r2s, xzs)):
        m = lax.rem(lon + (n - 1 - s), n)
        there = block_of(m)
        for level in range(share):
            for block in range(n):
                cols = slice(block * LANES, (block + 1) * LANES)
                place = level * n + block
                for pair in range(2):
                    far = xz[pair * LEVELS + place]
                    for second in range(2):
                        f = 2 * pair + second
                        if second:
                            far = roll(far, ROWS // 2, 0)
                        dyn[f, m * share + level, :ROWS, cols] = x[f * LEVELS + place]
                        dyn[f, m * share + level, ROWS:, cols] = halo(r2[f * LEVELS + place], far)
        for k in range(LEVELS):
            far = xz[DYN2 + k]
            mix[0, k, :ROWS, there] = x[CHL + k]
            mix[1, k, :ROWS, there] = x[SUM + k]
            mix[0, k, ROWS:, there] = halo(r2[CHL + k], far)
            mix[1, k, ROWS:, there] = halo(r2[SUM + k], roll(far, ROWS // 2, 0))
        edge0[m] = x[EDGE : EDGE + LEVELS]
        a, d = xz[MIX2] * keep_z, [r2[EDGE : EDGE + LEVELS, row, :] for row in (0, ROWS - 1)]
        corner[m, 0] = jnp.where(upper, d[1], a)
        corner[m, 1] = jnp.where(upper, a, d[0])

    wide = (2 * ROWS, width)
    col = iota(wide, 1)
    ring = iota(wide, 0)
    row = strip * ROWS + jnp.where(ring < ROWS + ROWS // 2, ring, ring - 2 * ROWS)
    fcor = 2.0 * (row.astype(jnp.float32) + 0.5) / (strips * ROWS) - 1.0
    not_last = col < width - 1
    not_first = col > 0

    def east(q):
        return jnp.where(not_last, roll(q, -1, 1), 0.0)

    def west(q):
        return jnp.where(not_first, roll(q, 1, 1), 0.0)

    def north(q):
        return roll(q, -1, 0)

    def south(q):
        return roll(q, 1, 0)

    def lap(q, e, nn):
        return e + west(q) + nn + south(q) - 4.0 * q

    def one_level(k, carry):
        uu, vv, tt, heat = dyn[0, k], dyn[1, k], dyn[2, k], dyn[3, k]
        chl, total = mix[0, k], mix[1, k]
        wet = (depth[...] > k.astype(jnp.float32)).astype(jnp.float32)
        wet_u, wet_v = wet * east(wet), wet * north(wet)
        new = []
        for step in range(STEPS):
            tau, top = carry[2 * step], carry[2 * step + 1]
            te, tn = east(tt), north(tt)
            u_new = wet_u * (
                uu + 0.1 * lap(uu, east(uu), north(uu)) + 0.3 * fcor * vv - 0.2 * (te - tt)
            )
            v_new = wet_v * (
                vv + 0.1 * lap(vv, east(vv), north(vv)) - 0.3 * fcor * uu - 0.2 * (tn - tt)
            )
            tt = wet * (tt + 0.1 * lap(tt, te, tn) + 0.5 * heat)
            uu, vv = u_new, v_new
            uw, vs = west(uu), south(vv)
            a0 = 1.0 - 0.5 * (
                (jnp.maximum(uu, 0.0) - jnp.minimum(uw, 0.0)) + (jnp.maximum(vv, 0.0) - jnp.minimum(vs, 0.0))
            )
            ae, aw = -0.5 * jnp.minimum(uu, 0.0), 0.5 * jnp.maximum(uw, 0.0)
            an, a_s = -0.5 * jnp.minimum(vv, 0.0), 0.5 * jnp.maximum(vs, 0.0)

            def advect(q):
                return a0 * q + (ae * east(q) + aw * west(q)) + (an * north(q) + a_s * south(q))

            moved = advect(chl)
            tau = tau + (0.1 + 0.3 * jnp.maximum(moved, 0.0))
            below = jnp.exp(-tau)
            heat = 2.0 * wet * (top - below)
            share_of_light = 0.5 * wet * top
            for i, q in enumerate((a0, ae, aw, an, a_s, wet, share_of_light)):
                coef[step, i, k] = q
            if step + 1 < STEPS:
                chl = wet * moved + share_of_light * advect(total)
            new += [tau, below]
        out4[0, k], out4[1, k], out4[2, k], out4[3, k] = uu[:ROWS], vv[:ROWS], tt[:ROWS], heat[:ROWS]
        return tuple(new)

    zero, one = jnp.zeros(wide, jnp.float32), jnp.ones(wide, jnp.float32)
    lax.fori_loop(0, LEVELS, one_level, (zero, one) * STEPS)
    mine = pl.ds(lon * share, share)
    for i, ref in enumerate((u_out, v_out, t_out, h_out)):
        ref[...] = out4[i, mine]

    kind = lane % 4
    lon_e, lon_w = jnp.minimum(lon + 1, n - 1), jnp.maximum(lon - 1, 0)
    to_east = jnp.where(lon < n - 1, 1.0, 0.0)
    to_west = jnp.where(lon > 0, 1.0, 0.0)
    exists = jnp.where(kind >= 2, to_east, to_west)
    easterly = kind >= 2

    def swapped(q):
        return jnp.where(kind == 1, roll(q, -1, 1), roll(q, 1, 1))

    def beside(edge, q, b):
        cols = roll(edge, LANES - 2 - 4 * b, 1)
        return (
            jnp.where(lane == LANES - 1, cols, roll(q, -1, 1)),
            jnp.where(lane == 0, cols, roll(q, 1, 1)),
        )

    def tile_coef(step, i, k):
        return coef[step, i, k, :ROWS, here]

    corners = []
    for side in range(2):
        q = jnp.where(easterly, corner[lon_e, side], corner[lon_w, side]) * exists
        corners.append(q)
    east_block, west_block = block_of(lon_e), block_of(lon_w)
    ends = []
    ends_raw = []
    for k in range(LEVELS):
        q = jnp.where(easterly, edge0[lon_e, k], edge0[lon_w, k]) * exists
        ends_raw.append(q)
        mid[0, k] = swapped(q)
    row_n, row_s = corners[1], corners[0]
    edge1[1, :, ROWS - 1, :] = row_n
    edge1[1, :, 0, :] = row_s
    for k in range(LEVELS):
        q = ends_raw[k]
        mine_edge = own[EDGE + k]
        outer = jnp.where(easterly, roll(q, -1, 1), roll(q, 1, 1))
        inner = jnp.where(easterly, roll(mine_edge, 1, 1), roll(mine_edge, -1, 1))
        rim = edge1[1, k]
        up = jnp.where(sub == ROWS - 1, rim, roll(q, -1, 0))
        down = jnp.where(sub == 0, rim, roll(q, 1, 0))

        def at_edge(i):
            e = jnp.broadcast_to(coef[0, i, k, :ROWS, east_block][:, :1], (ROWS, LANES))
            w = jnp.broadcast_to(coef[0, i, k, :ROWS, west_block][:, LANES - 1 :], (ROWS, LANES))
            return e, w

        a0, ae, aw, an, a_s, wet, light = (at_edge(i) for i in range(7))

        def pick(pair):
            return jnp.where(easterly, pair[0], pair[1])

        out_c = jnp.where(easterly, ae[0], aw[1])
        in_c = jnp.where(easterly, aw[0], ae[1])
        ends.append(
            (pick(a0) * q + (out_c * outer + in_c * inner) + (pick(an) * up + pick(a_s) * down), pick(wet), pick(light))
        )
    moved = jnp.concatenate([e[0] for e in ends], axis=0)
    react = exact_product(split(moved), (e_high[...], e_low[...]))
    for k in range(LEVELS):
        q, wet, light = ends[k]
        mid[1, k] = swapped((wet * q + light * react[k * ROWS : (k + 1) * ROWS]) * exists)

    m_pair = (m_high[...], m_low[...])
    for side, (at, ring_row) in enumerate(((0, 2 * ROWS - 1), (ROWS - 1, ROWS))):
        a0, ae, aw, an, a_s, wet, light = (coef[0, i, :, ring_row, here] for i in range(7))
        rim = swapped(corners[side])
        for b in range(tracers):
            q, q2 = near_rows(b, 0)[side], near_rows(b, 1)[side]
            row0[b, :, at, :] = q
            inner = c[b, :, at, :]
            e, w = beside(rim, q, b)
            up, down = (inner, q2) if side == 0 else (q2, inner)
            adv[b * ROWS : (b + 1) * ROWS, side * LANES : (side + 1) * LANES] = (
                a0 * q + (ae * e + aw * w) + (an * up + a_s * down)
            )
    react = exact_product(m_pair, split(adv[...]))
    for side, (at, ring_row) in enumerate(((0, 2 * ROWS - 1), (ROWS - 1, ROWS))):
        wet, light = (coef[0, i, :, ring_row, here] for i in (5, 6))
        for b in range(tracers):
            part = (slice(b * ROWS, (b + 1) * ROWS), slice(side * LANES, (side + 1) * LANES))
            row1[b, :, at, :] = wet * adv[part] + light * react[part]

    for step, (source, rows_ref, target) in enumerate(((c, row0, c_out), (c_out, row1, c_out))):

        def two_levels(i, carry, step=step, source=source, rows_ref=rows_ref, target=target):
            for half in range(2):
                k = 2 * i + half
                a0, ae, aw, an, a_s = (tile_coef(step, j, k) for j in range(5))
                edge = mid[step, k]
                for b in range(tracers):
                    q, rim = source[b, k], rows_ref[b, k]
                    e, w = beside(edge, q, b)
                    up = jnp.where(sub == ROWS - 1, rim, roll(q, -1, 0))
                    down = jnp.where(sub == 0, rim, roll(q, 1, 0))
                    adv[b * ROWS : (b + 1) * ROWS, half * LANES : (half + 1) * LANES] = (
                        a0 * q + (ae * e + aw * w) + (an * up + a_s * down)
                    )
            react = exact_product(m_pair, split(adv[...]))
            for half in range(2):
                k = 2 * i + half
                wet, light = tile_coef(step, 5, k), tile_coef(step, 6, k)
                for b in range(tracers):
                    part = (slice(b * ROWS, (b + 1) * ROWS), slice(half * LANES, (half + 1) * LANES))
                    target[b, k] = wet * adv[part] + light * react[part]
            return carry

        lax.fori_loop(0, LEVELS // 2, two_levels, 0)


def shards(n, lats, u, v, t, h, c, count, rates):
    tracers = c.shape[0]
    share, width = u.shape[0], u.shape[2]
    strips = lats * CORES
    lat, lon, role = lax.axis_index("lat"), lax.axis_index("lon"), lax.axis_index("role")
    pos = jnp.stack([lat * CORES + role, lon, role]).astype(jnp.int32)
    vmem = pl.BlockSpec(memory_space=pltpu.VMEM)
    smem = pl.BlockSpec(memory_space=pltpu.SMEM)
    params = pltpu.CompilerParams(vmem_limit_bytes=48 * 1024 * 1024)
    f32 = jnp.float32

    def tiles(count):
        return jax.ShapeDtypeStruct((count, ROWS, LANES), f32)

    z_tiles = DYN2 + n + 2 * (tracers + 1)
    x_pay, z_pay, r_pay, xz_pay = pl.pallas_call(
        functools.partial(pack_kernel, n),
        out_shape=(tiles(X_TILES), tiles(z_tiles), tiles(z_tiles), tiles(XZ_TILES)),
        in_specs=[smem, smem] + [vmem] * 6,
        out_specs=(vmem,) * 4,
        compiler_params=params,
        name="pack",
    )(pos, rates, u, v, t, h, count, c)

    def permute(q, target):
        pairs = []
        for a in range(lats):
            for o in range(n):
                for i in range(CORES):
                    a2, o2, i2 = target(a, o, i)
                    pairs.append(((a * n + o) * CORES + i, (a2 * n + o2) * CORES + i2))
        return lax.ppermute(q, ("lat", "lon", "role"), pairs)

    def over_lat(a, i):
        s = a * CORES + i + (1 if i else -1)
        return (s // CORES, s % CORES) if 0 <= s < strips else None

    def z_target(a, o, i):
        to = over_lat(a, i)
        return (to[0], o, to[1]) if to else (a, o ^ 1 if o ^ 1 < n else o, i)

    def shifted(shift):
        def x_target(a, o, i):
            return a, (o + shift) % n, i

        def xz_target(a, o, i):
            to = over_lat(a, i) or (a, i)
            return to[0], (o + shift) % n, to[1]

        return x_target, xz_target

    def across(a, o, i):
        return a, o, 1 - i

    z_in = permute(z_pay, z_target)
    xs, xzs = [], []
    for shift in range(1, n):
        x_target, xz_target = shifted(shift)
        xs.append(permute(x_pay, x_target))
        xzs.append(permute(xz_pay, xz_target))
    r_in = permute(r_pay, across)
    r2s = [permute(x, across) for x in xs]

    m_size, e_size = tracers * ROWS, LANES
    spread = pl.pallas_call(
        spread_kernel,
        out_shape=tuple(jax.ShapeDtypeStruct((s, s), jnp.bfloat16) for s in (m_size, m_size, e_size, e_size)),
        in_specs=[vmem],
        out_specs=(vmem,) * 4,
        compiler_params=params,
        name="spread",
    )(rates)

    whole = jax.ShapeDtypeStruct(u.shape, f32)
    args = (pos, u, v, t, h, count, c, x_pay, *spread, z_in, r_in, *xs, *r2s, *xzs)
    u, v, t, h, c = pl.pallas_call(
        functools.partial(step_kernel, n, strips),
        out_shape=(whole,) * 4 + (jax.ShapeDtypeStruct(c.shape, f32),),
        in_specs=[smem] + [vmem] * (len(args) - 1),
        out_specs=(vmem,) * 5,
        scratch_shapes=[
            pltpu.VMEM((FIELDS, LEVELS, 2 * ROWS, width), f32),
            pltpu.VMEM((2, LEVELS, 2 * ROWS, width), f32),
            pltpu.VMEM((2 * ROWS, width), f32),
            pltpu.VMEM((STEPS, 7, LEVELS, 2 * ROWS, width), f32),
            pltpu.VMEM((tracers, LEVELS, ROWS, LANES), f32),
            pltpu.VMEM((tracers, LEVELS, ROWS, LANES), f32),
            pltpu.VMEM((n, LEVELS, ROWS, LANES), f32),
            pltpu.VMEM((n, 2, LEVELS, LANES), f32),
            pltpu.VMEM((2, LEVELS, ROWS, LANES), f32),
            pltpu.VMEM((tracers * ROWS, 2 * LANES), f32),
            pltpu.VMEM((2, LEVELS, ROWS, LANES), f32),
            pltpu.VMEM((FIELDS, LEVELS, ROWS, width), f32),
        ],
        compiler_params=params,
        name="steps",
    )(*args)
    return u, v, t, h, c


def solution(mesh):
    level = P("lon", ("grp", "lat", "role"), None)
    tracer = P(None, None, ("grp", "lat", "role"), "lon")
    return jax.shard_map(
        functools.partial(shards, mesh.shape["lon"], mesh.shape["lat"]),
        mesh=mesh,
        in_specs=(level, level, level, level, tracer, P(("grp", "lat", "role"), None), P()),
        out_specs=(level, level, level, level, tracer),
        check_vma=False,
    )
```

```python
import functools

import jax
import jax.numpy as jnp
from jax import lax
from jax.experimental import pallas as pl
from jax.experimental.pallas import tpu as pltpu
from jax.sharding import PartitionSpec as P

ROWS = 8
LANES = 128
LEVELS = 8
CORES = 2
FIELDS = 4
NEAR = 4

RING_ROWS = 2 * ROWS
RING_COLS = 2 * LANES


def iota(shape, dim):
    return lax.broadcasted_iota(jnp.int32, shape, dim)


def roll(q, shift, axis):
    return pltpu.roll(q, shift % q.shape[axis], axis)


def block_of(m):
    return pl.ds(pl.multiple_of(m * LANES, LANES), LANES)


def load_kernel(n, pos, u, v, t, h, count, c, f_out, c_out, d_out, z_out, r_out, f_sem, c_sem):
    tracers = c.shape[0]
    share = f_out.shape[1]
    copies = [pltpu.make_async_copy(ref, f_out.at[i], f_sem.at[i]) for i, ref in enumerate((u, v, t, h))]
    copies.append(pltpu.make_async_copy(count, d_out, f_sem.at[FIELDS]))
    batch = tracers // c_sem.shape[0]
    c_copies = []
    for i in range(c_sem.shape[0]):
        part = pl.ds(i * batch, batch)
        c_copies.append(pltpu.make_async_copy(c.at[part], c_out.at[part], c_sem.at[i]))
    for copy in copies + c_copies:
        copy.start()
    upper = pos[2] == 1
    to_z = (iota((ROWS, LANES), 0) >= ROWS // 2) == upper
    for copy in copies:
        copy.wait()
    for level in range(share):
        for block in range(n):
            cols = slice(block * LANES, (block + 1) * LANES)
            place = level * n + block
            for pair in range(2):
                a = f_out[2 * pair, level, :, cols]
                b = roll(f_out[2 * pair + 1, level, :, cols], ROWS // 2, 0)
                z_out[pair * LEVELS + place] = jnp.where(to_z, a, b)
                r_out[pair * LEVELS + place] = jnp.where(to_z, b, a)
    base = 2 * LEVELS
    for block in range(n):
        depth = d_out[:, block * LANES : (block + 1) * LANES].astype(jnp.float32)
        z_out[base + block] = depth
        r_out[base + block] = depth
    base += n
    for i, copy in enumerate(c_copies):
        copy.wait()
        for b in range(i * batch, (i + 1) * batch):
            for far in range(2):
                bottom, top = c_out[b, :, far, :], c_out[b, :, ROWS - 1 - far, :]
                z_out[base + 2 * b + far] = jnp.where(upper, top, bottom)
                r_out[base + 2 * b + far] = jnp.where(upper, bottom, top)


def pack_kernel(n, pos, rates, f, c, r, *outs):
    sums, edges = outs[:2]
    x_outs, xz_outs = outs[2 : 1 + n], outs[1 + n :]
    tracers, share = c.shape[0], f.shape[1]
    lon, upper = pos[1], pos[2] == 1
    to_z = (iota((ROWS, LANES), 0) >= ROWS // 2) == upper
    lane = iota((ROWS, LANES), 1)

    def packed(get):
        total = jnp.zeros((ROWS, LANES), jnp.float32)
        edge = jnp.zeros((ROWS, LANES), jnp.float32)
        for b in range(tracers):
            q = get(b)
            total = total + rates[0, b] * q
            edge = jnp.where(lane // 4 == b, roll(q, 4 * b + 2, 1), edge)
        return total, jnp.where(lane // 4 == tracers, roll(total, 4 * tracers + 2, 1), edge)

    def one_level(k, carry):
        sums[k], edges[k] = packed(lambda b: c[b, k])
        return carry

    lax.fori_loop(0, LEVELS, one_level, 0)
    base = 2 * LEVELS + n
    _, corner = packed(lambda b: r[base + 2 * b])
    count = FIELDS * share
    for s, (x_out, xz_out) in enumerate(zip(x_outs, xz_outs)):
        m = lax.rem(lon + (s + 1), n)
        e, w = lax.rem(m + 1, n), lax.rem(m + n - 1, n)

        def sides_of(get, amount):
            sides = jnp.zeros((ROWS, LANES), jnp.float32)
            for i in range(amount):
                side = jnp.where(lane < LANES // 2, get(i, e), get(i, w))
                sides = jnp.where(lane // (2 * NEAR) == i, roll(side, 2 * NEAR * i + NEAR, 1), sides)
            return sides

        def whole(i, block):
            return f[i // share, i % share, :, block_of(block)]

        def outgoing(i, block):
            pair, level = i // share, i % share
            a, b = f[2 * pair, level, :, block_of(block)], f[2 * pair + 1, level, :, block_of(block)]
            return jnp.where(to_z, a, roll(b, ROWS // 2, 0))

        def beside(i, block):
            return r[(i // share) * LEVELS + (i % share) * n + block]

        x_out[count + 1 : count + 1 + LEVELS] = edges[...]
        end = count + 1 + LEVELS
        for i in range(count):
            x_out[i] = whole(i, m)
        for i in range(count // 2):
            x_out[end + i] = beside(i, m)
            xz_out[i] = outgoing(i, m)
        x_out[count] = sides_of(whole, count)
        x_out[end + count // 2] = sides_of(beside, count // 2)
        x_out[end + count // 2 + 1] = corner
        xz_out[count // 2] = sides_of(outgoing, count // 2)
        xz_out[count // 2 + 1] = jnp.where(upper, edges[:, ROWS - 1, :], edges[:, 0, :])


def split(q):
    high = q.astype(jnp.bfloat16)
    return high, (q - high.astype(jnp.float32)).astype(jnp.bfloat16)


def spread_kernel(rates, m_high, m_low, e_high, e_low):
    tracers = rates.shape[0]
    exact = functools.partial(jnp.dot, precision=lax.Precision.HIGHEST, preferred_element_type=jnp.float32)
    for group, transposed, high, low in ((ROWS, False, m_high, m_low), (4, True, e_high, e_low)):
        size = high.shape[0]
        rows = (iota((size, tracers), 0) // group == iota((size, tracers), 1)).astype(jnp.float32)
        cols = (iota((tracers, size), 1) // group == iota((tracers, size), 0)).astype(jnp.float32)
        wide = exact(exact(rows, rates[...].T if transposed else rates[...]), cols)
        same = iota((size, size), 0) % group == iota((size, size), 1) % group
        high[...], low[...] = split(jnp.where(same, wide, 0.0))


def exact_product(left, right):
    dot = functools.partial(jnp.dot, preferred_element_type=jnp.float32)
    return dot(left[0], right[0]) + (dot(left[0], right[1]) + dot(left[1], right[0]))


class Halo:
    def __init__(self, pos, strips):
        self.upper = pos[2] == 1
        end = jnp.logical_or(
            jnp.logical_and(pos[0] == 0, jnp.logical_not(self.upper)),
            jnp.logical_and(pos[0] == strips - 1, self.upper),
        )
        self.keep_z = jnp.where(end, 0.0, 1.0)
        self.from_r = (iota((ROWS, LANES), 0) >= ROWS // 2) == self.upper

    def rows(self, r, z):
        return jnp.where(self.from_r, r, z * self.keep_z)

    def sides(self, r, z):
        z = z * self.keep_z
        return jnp.where(self.upper, r, z), jnp.where(self.upper, z, r)


def flow_kernel(n, strips, *refs):
    pos, rates, f, count, c, sums, edges, z, r = refs[:9]
    others = n - 1
    xs, xzs = (refs[9 + i * others : 9 + (i + 1) * others] for i in range(2))
    coef1, coef2, ends, rims, f_out = refs[9 + 2 * others : 14 + 2 * others]
    heats = refs[14 + 2 * others : 14 + 3 * others]
    dyn, mix, depth, all_edges, all_rims, out, light_out = refs[14 + 3 * others :]
    tracers, share = c.shape[0], f.shape[1]
    strip, lon = pos[0], pos[1]
    halo = Halo(pos, strips)
    lane = iota((ROWS, LANES), 1)
    first, second = slice(0, LANES), slice(LANES, RING_COLS)
    own_rows, next_rows = slice(0, ROWS), slice(ROWS, RING_ROWS)
    base = 2 * LEVELS + n
    half = ROWS // 2

    def beside(m):
        return lax.rem(m + 1, n), lax.rem(m + n - 1, n)

    def window(main, near, m):
        east, west = beside(m)

        def side(g):
            return g(east) if n == 2 else jnp.where(lane < LANES // 2, g(east), g(west))

        return main(m), side(main), near(m), side(near)

    def put(ref, at, tiles):
        for tile, (rows, cols) in zip(
            tiles, ((own_rows, first), (own_rows, second), (next_rows, first), (next_rows, second))
        ):
            ref[(*at, rows, cols)] = tile

    def own_window(field, level, m):
        pair, odd = field // 2, field % 2

        def near(block):
            place = pair * LEVELS + level * n + block
            a, b = r[place], z[place]
            if odd:
                a, b = roll(a, half, 0), roll(b, half, 0)
            return halo.rows(a, b)

        return window(lambda block: f[field, level, :, block_of(block)], near, m)

    for field in range(FIELDS):
        for level in range(share):
            put(dyn, (field, lon * share + level), own_window(field, level, lon))

    def depth_window(m):
        return window(
            lambda block: count[:, block_of(block)].astype(jnp.float32),
            lambda block: halo.rows(r[2 * LEVELS + block], z[2 * LEVELS + block]),
            m,
        )

    put(depth, (), depth_window(lon))

    sides = FIELDS * share
    end = sides + 1 + LEVELS
    for s, (x, xz) in enumerate(zip(xs, xzs)):
        m = lax.rem(lon + (n - 1 - s), n)
        for field in range(FIELDS):
            for level in range(share):
                i, j = field * share + level, (field // 2) * share + level
                shift = -(2 * NEAR * j + NEAR)
                near = [x[end + j], xz[j], roll(x[end + sides // 2], shift, 1), roll(xz[sides // 2], shift, 1)]
                if field % 2:
                    near = [roll(q, half, 0) for q in near]
                side = roll(x[sides], -(2 * NEAR * i + NEAR), 1)
                put(
                    dyn,
                    (field, m * share + level),
                    (x[i], side, halo.rows(near[0], near[1]), halo.rows(near[2], near[3])),
                )
        all_edges[m] = x[sides + 1 : end]
        all_rims[m, 0], all_rims[m, 1] = halo.sides(x[end + sides // 2 + 1], xz[sides // 2 + 1])

    east, west = beside(lon)
    easterly = lane % 4 >= 2
    exists = jnp.where(easterly, jnp.where(lon < n - 1, 1.0, 0.0), jnp.where(lon > 0, 1.0, 0.0))
    for k in range(LEVELS):
        ends[k] = jnp.where(easterly, all_edges[east, k], all_edges[west, k]) * exists
    for side in range(2):
        rims[side] = jnp.where(easterly, all_rims[east, side], all_rims[west, side]) * exists

    mix[0, :, own_rows, first] = c[0]
    mix[1, :, own_rows, first] = sums[...]
    for i, b in enumerate((0, tracers)):
        for k in range(LEVELS):
            mix[i, k, own_rows, second] = roll(ends[k], -(4 * b + 2), 1)
        for side, place in enumerate((RING_ROWS - 1, ROWS)):
            mix[i, :, place, second] = roll(rims[side], -(4 * b + 2), 1)
    for far in range(2):
        total = [jnp.zeros((LEVELS, LANES), jnp.float32)] * 2
        for b in range(tracers):
            rows = halo.sides(r[base + 2 * b + far], z[base + 2 * b + far])
            if b == 0:
                chl = rows
            total = [a + rates[0, b] * q for a, q in zip(total, rows)]
        for i, rows in enumerate((chl, total)):
            mix[i, :, RING_ROWS - 1 - far, first] = rows[0]
            mix[i, :, ROWS + far, first] = rows[1]

    wide = (RING_ROWS, RING_COLS)
    ring_row, ring_col = iota(wide, 0), iota(wide, 1)
    row = strip * ROWS + jnp.where(ring_row < ROWS + half, ring_row, ring_row - RING_ROWS)
    fcor = 2.0 * (row.astype(jnp.float32) + 0.5) / (strips * ROWS) - 1.0

    def north(q):
        return roll(q, -1, 0)

    def south(q):
        return roll(q, 1, 0)

    def around(m):
        e, w = beside(m)
        block = jnp.where(ring_col < LANES, m, jnp.where(ring_col < LANES + LANES // 2, e, w))
        col = block * LANES + ring_col % LANES
        not_last, not_first = col < n * LANES - 1, col > 0
        return (
            lambda q: jnp.where(not_last, roll(q, -1, 1), 0.0),
            lambda q: jnp.where(not_first, roll(q, 1, 1), 0.0),
        )

    def masks(k, counts, east):
        wet = jnp.where(counts > k.astype(jnp.float32), 1.0, 0.0)
        return wet, wet * east(wet), wet * north(wet)

    def advance(uu, vv, tt, wets, east, west):
        wet, wet_u, wet_v = wets

        def lap(q, e, nn):
            return e + west(q) + nn + south(q) - 4.0 * q

        te, tn = east(tt), north(tt)
        u_new = wet_u * (uu + 0.1 * lap(uu, east(uu), north(uu)) + 0.3 * fcor * vv - 0.2 * (te - tt))
        v_new = wet_v * (vv + 0.1 * lap(vv, east(vv), north(vv)) - 0.3 * fcor * uu - 0.2 * (tn - tt))
        return u_new, v_new, wet * (tt + 0.1 * lap(tt, te, tn))

    def coefficients(uu, vv, uw, vs):
        a0 = 1.0 - 0.5 * (
            (jnp.maximum(uu, 0.0) - jnp.minimum(uw, 0.0)) + (jnp.maximum(vv, 0.0) - jnp.minimum(vs, 0.0))
        )
        return (
            a0,
            -0.5 * jnp.minimum(uu, 0.0),
            0.5 * jnp.maximum(uw, 0.0),
            -0.5 * jnp.minimum(vv, 0.0),
            0.5 * jnp.maximum(vs, 0.0),
        )

    east_of, west_of = around(lon)

    def one_level(k, carry):
        tau1, top1, tau2, top2 = carry
        wets = masks(k, depth[...], east_of)
        wet = wets[0]
        heat0 = dyn[3, k]
        uu, vv, tt = advance(dyn[0, k], dyn[1, k], dyn[2, k], wets, east_of, west_of)
        tt = tt + 0.5 * (wet * heat0)
        stencil = coefficients(uu, vv, west_of(uu), south(vv))

        def advect(q):
            a0, ae, aw, an, a_s = stencil
            return a0 * q + (ae * east_of(q) + aw * west_of(q)) + (an * north(q) + a_s * south(q))

        moved = advect(mix[0, k])
        tau1 = tau1 + (0.1 + 0.3 * jnp.maximum(moved, 0.0))
        below = jnp.exp(-tau1)
        half_wet = 0.5 * wet
        warm = half_wet * (2.0 * (top1 - below))
        light = half_wet * top1
        for i, q in enumerate((*stencil, wet, light)):
            coef1[i, k] = q
        chl = wet * moved + light * advect(mix[1, k])
        top1 = below

        uu, vv, tt = advance(uu, vv, tt, wets, east_of, west_of)
        inner = (own_rows, first)
        own = [q[inner] for q in coefficients(uu, vv, west_of(uu), south(vv))]
        moved = (
            own[0] * chl[inner]
            + (own[1] * east_of(chl)[inner] + own[2] * west_of(chl)[inner])
            + (own[3] * north(chl)[inner] + own[4] * south(chl)[inner])
        )
        tau2 = tau2 + (0.1 + 0.3 * jnp.maximum(moved, 0.0))
        below = jnp.exp(-tau2)
        for i, q in enumerate((*own, wet[inner], half_wet[inner] * top2)):
            coef2[i, k] = q
        light_out[0, k] = warm[inner]
        light_out[1, k] = 2.0 * wet[inner] * (top2 - below)
        out[0, k], out[1, k], out[2, k] = uu[own_rows], vv[own_rows], tt[own_rows]
        return tau1, top1, tau2, below

    big = jnp.zeros(wide, jnp.float32)
    small = jnp.zeros((ROWS, LANES), jnp.float32)
    lax.fori_loop(0, LEVELS, one_level, (big, big + 1.0, small, small + 1.0))

    here = block_of(lon)
    for level in range(share):
        k = lon * share + level
        for i in range(3):
            q = out[i, k, :, first]
            f_out[i, level, :, here] = q + light_out[0, k] if i == 2 else q
            if n == 2:
                f_out[i, level, :, block_of(1 - lon)] = out[i, k, :, second]
        f_out[3, level, :, here] = light_out[1, k]
    for s, heat in enumerate(heats):
        m = lax.rem(lon + (s + 1), n)
        for i in range(2):
            heat[i] = light_out[i, pl.ds(m * share, share)]

    if n > 2:

        def other_block(s, carry):
            m = lax.rem(lon + s, n)
            e, w = around(m)
            put(depth, (), depth_window(m))
            for level in range(share):
                k = lon * share + level
                wets = masks(k, depth[...], e)
                for field in range(FIELDS):
                    put(dyn, (field, k), own_window(field, level, m))
                uu, vv, tt = advance(dyn[0, k], dyn[1, k], dyn[2, k], wets, e, w)
                tt = tt + 0.5 * (wets[0] * dyn[3, k])
                for i, q in enumerate(advance(uu, vv, tt, wets, e, w)):
                    f_out[i, level, :, block_of(m)] = q[own_rows, first]
            return carry

        lax.fori_loop(1, n, other_block, 0)


def tile_stencil(q, rim, columns, stencil, sub, lane):
    a0, ae, aw, an, a_s = stencil
    e = jnp.where(lane == LANES - 1, columns, roll(q, -1, 1))
    w = jnp.where(lane == 0, columns, roll(q, 1, 1))
    up = jnp.where(sub == ROWS - 1, rim, roll(q, -1, 0))
    down = jnp.where(sub == 0, rim, roll(q, 1, 0))
    return a0 * q + (ae * e + aw * w) + (an * up + a_s * down)


def swapped(q):
    return jnp.where(iota(q.shape, 1) % 4 == 1, roll(q, -1, 1), roll(q, 1, 1))


def beside_columns(edge, b):
    return roll(edge, LANES - 2 - 4 * b, 1)


def part_of(b, half):
    return slice(b * ROWS, (b + 1) * ROWS), slice(half * LANES, (half + 1) * LANES)


def tile_loop(source, rims, edge, coef, m_pair, adv, store):
    tracers = source.shape[0]
    sub, lane = iota((ROWS, LANES), 0), iota((ROWS, LANES), 1)

    def two_levels(i, carry):
        for half in range(2):
            k = 2 * i + half
            stencil = [coef(j, k) for j in range(5)]
            columns = edge[k]
            for b in range(tracers):
                adv[part_of(b, half)] = tile_stencil(
                    source[b, k], rims[b, k], beside_columns(columns, b), stencil, sub, lane
                )
        react = exact_product(m_pair, split(adv[...]))
        for half in range(2):
            k = 2 * i + half
            wet, light = coef(5, k), coef(6, k)
            for b in range(tracers):
                store(b, k, wet * adv[part_of(b, half)] + light * react[part_of(b, half)])
        return carry

    return two_levels


def first_kernel(n, strips, pos, c, edges, ends, rims, coef, m_high, m_low, e_high, e_low, z, r, c_out, row1, edge1, row0, edge0, adv):
    tracers = c.shape[0]
    lon = pos[1]
    halo = Halo(pos, strips)
    sub, lane = iota((ROWS, LANES), 0), iota((ROWS, LANES), 1)
    easterly = lane % 4 >= 2
    base = 2 * LEVELS + n
    m_pair = (m_high[...], m_low[...])

    rim = row0.at[0]
    rim[:, 0, :] = rims[0]
    rim[:, ROWS - 1, :] = rims[1]
    parts = []
    for k in range(LEVELS):
        q, inside = ends[k], edges[k]
        outer = jnp.where(easterly, roll(q, -1, 1), roll(q, 1, 1))
        inner = jnp.where(easterly, roll(inside, 1, 1), roll(inside, -1, 1))
        up = jnp.where(sub == ROWS - 1, rim[k], roll(q, -1, 0))
        down = jnp.where(sub == 0, rim[k], roll(q, 1, 0))

        def at_edge(i):
            side = coef[i, k, :ROWS, LANES:]
            return (
                jnp.broadcast_to(side[:, :1], (ROWS, LANES)),
                jnp.broadcast_to(side[:, LANES - 1 :], (ROWS, LANES)),
            )

        def pick(pair):
            return jnp.where(easterly, pair[0], pair[1])

        a0, ae, aw, an, a_s, wet, light = (at_edge(i) for i in range(7))
        moved = (
            pick(a0) * q
            + (pick((ae[0], aw[1])) * outer + pick((aw[0], ae[1])) * inner)
            + (pick(an) * up + pick(a_s) * down)
        )
        parts.append((moved, pick(wet), pick(light)))
        edge0[k] = swapped(q)
    react = exact_product(split(jnp.concatenate([p[0] for p in parts], axis=0)), (e_high[...], e_low[...]))
    east_exists = jnp.where(lon < n - 1, 1.0, 0.0)
    west_exists = jnp.where(lon > 0, 1.0, 0.0)
    exists = jnp.where(easterly, east_exists, west_exists)
    for k, (q, wet, light) in enumerate(parts):
        edge1[k] = swapped((wet * q + light * react[k * ROWS : (k + 1) * ROWS]) * exists)

    places = ((0, RING_ROWS - 1), (ROWS - 1, ROWS))
    corners = [swapped(rims[side]) for side in range(2)]
    stencils = [[coef[i, :, place, :LANES] for i in range(7)] for _, place in places]
    for b in range(tracers):
        near = halo.sides(r[base + 2 * b], z[base + 2 * b])
        far = halo.sides(r[base + 2 * b + 1], z[base + 2 * b + 1])
        for side, (at, _) in enumerate(places):
            a0, ae, aw, an, a_s, _, _ = stencils[side]
            q = near[side]
            row0[b, :, at, :] = q
            columns = beside_columns(corners[side], b)
            e = jnp.where(lane == LANES - 1, columns, roll(q, -1, 1))
            w = jnp.where(lane == 0, columns, roll(q, 1, 1))
            inner = c[b, :, at, :]
            up, down = (inner, far[side]) if side == 0 else (far[side], inner)
            adv[part_of(b, side)] = a0 * q + (ae * e + aw * w) + (an * up + a_s * down)
    react = exact_product(m_pair, split(adv[...]))
    for b in range(tracers):
        for side, (at, _) in enumerate(places):
            wet, light = stencils[side][5:]
            row1[b, :, at, :] = wet * adv[part_of(b, side)] + light * react[part_of(b, side)]

    def store(b, k, q):
        c_out[b, k] = q

    lax.fori_loop(
        0,
        LEVELS // 2,
        tile_loop(c, row0, edge0, lambda i, k: coef[i, k, :ROWS, :LANES], m_pair, adv, store),
        0,
    )


def last_kernel(n, *refs):
    others = n - 1
    pos, c, row1, edge1, coef, m_high, m_low, f = refs[:8]
    heats = refs[8 : 8 + others]
    u_out, v_out, t_out, h_out, c_out = refs[8 + others : 13 + others]
    result, warm, adv, sem, c_sem = refs[13 + others :]
    share = f.shape[1]
    lon = pos[1]
    flows = [pltpu.make_async_copy(f.at[i], ref, sem.at[i]) for i, ref in enumerate((u_out, v_out))]
    for copy in flows:
        copy.start()
    here = block_of(lon)
    for level in range(share):
        warm[0, level, :, here] = f[2, level, :, here]
        warm[1, level, :, here] = f[3, level, :, here]
        for s, heat in enumerate(heats):
            there = block_of(lax.rem(lon + (n - 1 - s), n))
            warm[0, level, :, there] = f[2, level, :, there] + heat[0, level]
            warm[1, level, :, there] = heat[1, level]
    flows += [pltpu.make_async_copy(warm.at[i], ref, sem.at[2 + i]) for i, ref in enumerate((t_out, h_out))]
    for copy in flows[2:]:
        copy.start()

    def store(b, k, q):
        result[b, k] = q

    def copy_out(i):
        part = pl.ds(2 * i, 2)
        return pltpu.make_async_copy(result.at[:, part], c_out.at[:, part], c_sem.at[i])

    body = tile_loop(c, row1, edge1, lambda i, k: coef[i, k], (m_high[...], m_low[...]), adv, store)

    def one_pass(i, carry):
        body(i, carry)
        copy_out(i).start()
        return carry

    lax.fori_loop(0, LEVELS // 2, one_pass, 0)
    for copy in flows:
        copy.wait()
    for i in range(LEVELS // 2):
        copy_out(i).wait()


def shards(n, lats, u, v, t, h, c, count, rates):
    tracers = c.shape[0]
    share, width = u.shape[0], u.shape[2]
    strips = lats * CORES
    lat, lon, role = lax.axis_index("lat"), lax.axis_index("lon"), lax.axis_index("role")
    pos = jnp.stack([lat * CORES + role, lon, role]).astype(jnp.int32)
    vmem = pl.BlockSpec(memory_space=pltpu.VMEM)
    smem = pl.BlockSpec(memory_space=pltpu.SMEM)
    anywhere = pl.BlockSpec(memory_space=pl.ANY)
    hbm = pl.BlockSpec(memory_space=pltpu.HBM)
    params = pltpu.CompilerParams(vmem_limit_bytes=32 * 1024 * 1024)
    dma = pltpu.SemaphoreType.DMA

    def shape(*dims, dtype=jnp.float32):
        return jax.ShapeDtypeStruct(dims, dtype)

    def tiles(*dims):
        return shape(*dims, ROWS, LANES)

    def scratch(*dims):
        return pltpu.VMEM(dims, jnp.float32)

    def call(kernel, name, args, in_specs, out_shape, out_specs=None, scratch_shapes=()):
        return pl.pallas_call(
            kernel,
            out_shape=tuple(out_shape),
            in_specs=in_specs,
            out_specs=out_specs or (vmem,) * len(out_shape),
            scratch_shapes=scratch_shapes,
            compiler_params=params,
            name=name,
        )(*args)

    def permute(q, target):
        pairs = []
        for a in range(lats):
            for o in range(n):
                for i in range(CORES):
                    a2, o2, i2 = target(a, o, i)
                    pairs.append(((a * n + o) * CORES + i, (a2 * n + o2) * CORES + i2))
        return lax.ppermute(q, ("lat", "lon", "role"), pairs)

    def over_lat(a, i):
        s = a * CORES + i + (1 if i else -1)
        return (s // CORES, s % CORES) if 0 <= s < strips else None

    def z_target(a, o, i):
        to = over_lat(a, i)
        return (to[0], o, to[1]) if to else (a, o ^ 1 if o ^ 1 < n else o, i)

    def x_target(shift):
        return lambda a, o, i: (a, (o + shift) % n, i)

    def xz_target(shift):
        def target(a, o, i):
            to = over_lat(a, i) or (a, i)
            return to[0], (o + shift) % n, to[1]

        return target

    def r_target(a, o, i):
        return a, o, 1 - i

    shifts = range(1, n)
    z_tiles = 2 * LEVELS + n + 2 * tracers
    xz_tiles = FIELDS * share // 2 + 2
    x_tiles = FIELDS * share + 1 + LEVELS + xz_tiles
    f, c_here, depth, z_pay, r_pay = call(
        functools.partial(load_kernel, n),
        "load",
        (pos, *(pltpu.with_memory_space_constraint(q, pltpu.HBM) for q in (u, v, t, h, count, c))),
        [smem] + [hbm] * 6,
        [
            shape(FIELDS, *u.shape),
            shape(*c.shape),
            shape(*count.shape, dtype=jnp.int32),
            tiles(z_tiles),
            tiles(z_tiles),
        ],
        scratch_shapes=[dma((FIELDS + 1,)), dma((4,))],
    )
    r_in = permute(r_pay, r_target)
    z_in = permute(z_pay, z_target)
    sums, edges, *pays = call(
        functools.partial(pack_kernel, n),
        "pack",
        (pos, rates, f, c_here, r_in),
        [smem, smem] + [vmem] * 3,
        [tiles(LEVELS)] * 2 + [tiles(x_tiles)] * (n - 1) + [tiles(xz_tiles)] * (n - 1),
    )
    xs = [permute(q, x_target(s)) for s, q in zip(shifts, pays[: n - 1])]
    xzs = [permute(q, xz_target(s)) for s, q in zip(shifts, pays[n - 1 :])]

    m_size, e_size = tracers * ROWS, LANES
    bf16 = jnp.bfloat16
    m_high, m_low, e_high, e_low = call(
        spread_kernel,
        "spread",
        (rates,),
        [vmem],
        [shape(s, s, dtype=bf16) for s in (m_size, m_size, e_size, e_size)],
    )

    args = (pos, rates, f, depth, c_here, sums, edges, z_in, r_in, *xs, *xzs)
    coef1, coef2, ends, rims, f_new, *heats = call(
        functools.partial(flow_kernel, n, strips),
        "flow",
        args,
        [smem, smem] + [vmem] * (len(args) - 2),
        [
            shape(7, LEVELS, RING_ROWS, RING_COLS),
            tiles(7, LEVELS),
            tiles(LEVELS),
            shape(2, LEVELS, LANES),
            shape(FIELDS, *u.shape),
        ]
        + [tiles(2, share)] * (n - 1),
        scratch_shapes=[
            scratch(FIELDS, LEVELS, RING_ROWS, RING_COLS),
            scratch(2, LEVELS, RING_ROWS, RING_COLS),
            scratch(RING_ROWS, RING_COLS),
            scratch(n, LEVELS, ROWS, LANES),
            scratch(n, 2, LEVELS, LANES),
            scratch(3, LEVELS, ROWS, RING_COLS),
            scratch(2, LEVELS, ROWS, LANES),
        ],
    )
    heats = [permute(q, x_target(s)) for s, q in zip(shifts, heats)]
    args = (pos, c_here, edges, ends, rims, coef1, m_high, m_low, e_high, e_low, z_in, r_in)
    c_mid, row1, edge1 = call(
        functools.partial(first_kernel, n, strips),
        "first",
        args,
        [smem] + [vmem] * (len(args) - 1),
        [shape(*c.shape), tiles(tracers, LEVELS), tiles(LEVELS)],
        scratch_shapes=[
            scratch(tracers, LEVELS, ROWS, LANES),
            scratch(LEVELS, ROWS, LANES),
            scratch(tracers * ROWS, 2 * LANES),
        ],
    )
    args = (pos, c_mid, row1, edge1, coef2, m_high, m_low, f_new, *heats)
    return call(
        functools.partial(last_kernel, n),
        "last",
        args,
        [smem] + [vmem] * (len(args) - 1),
        [shape(*u.shape)] * FIELDS + [shape(*c.shape)],
        out_specs=(anywhere,) * 5,
        scratch_shapes=[
            scratch(*c.shape),
            scratch(2, *u.shape),
            scratch(tracers * ROWS, 2 * LANES),
            dma((FIELDS,)),
            dma((LEVELS // 2,)),
        ],
    )


def solution(mesh):
    level = P("lon", ("grp", "lat", "role"), None)
    tracer = P(None, None, ("grp", "lat", "role"), "lon")
    return jax.shard_map(
        functools.partial(shards, mesh.shape["lon"], mesh.shape["lat"]),
        mesh=mesh,
        in_specs=(level, level, level, level, tracer, P(("grp", "lat", "role"), None), P()),
        out_specs=(level, level, level, level, tracer),
        check_vma=False,
    )
```

```python
import functools

import jax
import jax.numpy as jnp
from jax import lax
from jax.experimental import pallas as pl
from jax.experimental.pallas import tpu as pltpu
from jax.sharding import PartitionSpec as P

ROWS = 8
LANES = 128
LEVELS = 8
CORES = 2
FIELDS = 4
NEAR = 4

RING_ROWS = 2 * ROWS
RING_COLS = 2 * LANES


def iota(shape, dim):
    return lax.broadcasted_iota(jnp.int32, shape, dim)


def roll(q, shift, axis):
    return pltpu.roll(q, shift % q.shape[axis], axis)


def position():
    lat, lon, role = lax.axis_index("lat"), lax.axis_index("lon"), lax.axis_index("role")
    return lat * CORES + role, lon, role


def block_of(m):
    return pl.ds(pl.multiple_of(m * LANES, LANES), LANES)


def packed(tracers, rates, tiles):
    lane = iota((ROWS, LANES), 1)
    zero = jnp.zeros((ROWS, LANES), jnp.float32)
    total, edge = [zero] * len(tiles), [zero] * len(tiles)
    for b in range(tracers):
        rate = jnp.broadcast_to(rates[:1, b : b + 1], (ROWS, LANES))
        mine = lane // 4 == b
        for i, get in enumerate(tiles):
            q = get(b)
            total[i] = total[i] + rate * q
            edge[i] = jnp.where(mine, roll(q, 4 * b + 2, 1), edge[i])
    mine = lane // 4 == tracers
    return total, [jnp.where(mine, roll(t, 4 * tracers + 2, 1), e) for t, e in zip(total, edge)]


def last_rows(tiles):
    u, v, t, h = tiles
    sub = iota((ROWS, LANES), 0)
    low = jnp.where(sub >= 1, roll(t, -5, 0), roll(h, 1, 0))
    return jnp.where(sub >= 5, v, jnp.where(sub >= 3, roll(u, -3, 0), low))


def first_rows(tiles):
    u, v, t, h = tiles
    sub = iota((ROWS, LANES), 0)
    high = jnp.where(sub <= 6, roll(t, 5, 0), roll(h, -1, 0))
    return jnp.where(sub <= 2, v, jnp.where(sub <= 4, roll(u, 3, 0), high))


def next_rows(south, north, field):
    shift = (3, 0, 5, -1)[field]
    if shift:
        south, north = roll(south, shift, 0), roll(north, -shift, 0)
    return jnp.where(iota((ROWS, LANES), 0) >= ROWS // 2, south, north)


def sides_of(get, amount, east, west):
    lane = iota((ROWS, LANES), 1)
    sides = jnp.zeros((ROWS, LANES), jnp.float32)
    for i in range(amount):
        side = jnp.where(lane < LANES // 2, get(i, east), get(i, west))
        sides = jnp.where(lane // (2 * NEAR) == i, roll(side, 2 * NEAR * i + NEAR, 1), sides)
    return sides


def load_kernel(n, u, v, t, h, count, rates, c, f_out, c_out, d_out, rates_out, z_out, r_out, *refs):
    x_outs, xz_outs = refs[: n - 1], refs[n - 1 : 2 * (n - 1)]
    f_sem, c_sem = refs[2 * (n - 1) :]
    tracers, share = c.shape[0], f_out.shape[1]
    _, lon, role = position()
    upper = role == 1
    copies = [pltpu.make_async_copy(ref, f_out.at[i], f_sem.at[i]) for i, ref in enumerate((u, v, t, h))]
    copies.append(pltpu.make_async_copy(count, d_out, f_sem.at[FIELDS]))
    copies.append(pltpu.make_async_copy(rates, rates_out, f_sem.at[FIELDS + 1]))
    batch = tracers // c_sem.shape[0]
    c_copies = []
    for i in range(c_sem.shape[0]):
        part = pl.ds(i * batch, batch)
        c_copies.append(pltpu.make_async_copy(c.at[part], c_out.at[part], c_sem.at[i]))
    for copy in copies + c_copies:
        copy.start()
    for copy in copies:
        copy.wait()

    def whole(i, block):
        return f_out[i // share, i % share, :, block_of(block)]

    def strips_of(level, block):
        tiles = [whole(field * share + level, block) for field in range(FIELDS)]
        top, bottom = last_rows(tiles), first_rows(tiles)
        return jnp.where(upper, top, bottom), jnp.where(upper, bottom, top)

    count_f = FIELDS * share
    for level in range(share):
        for block in range(n):
            z_out[level * n + block], r_out[level * n + block] = strips_of(level, block)
    base = LEVELS
    for block in range(n):
        depth = d_out[:, block * LANES : (block + 1) * LANES].astype(jnp.float32)
        z_out[base + block] = depth
        r_out[base + block] = depth
    base += n
    for s, (x_out, xz_out) in enumerate(zip(x_outs, xz_outs)):
        m = lax.rem(lon + (s + 1), n)
        e, w = lax.rem(m + 1, n), lax.rem(m + n - 1, n)

        for i in range(count_f):
            x_out[i] = whole(i, m)
        for level in range(share):
            xz_out[level] = z_out[level * n + m]
        x_out[count_f] = sides_of(whole, count_f, e, w)
        xz_out[share] = sides_of(lambda level, block: z_out[level * n + block], share, e, w)
    for i, copy in enumerate(c_copies):
        copy.wait()
        for b in range(i * batch, (i + 1) * batch):
            for far in range(2):
                bottom, top = c_out[b, :, far, :], c_out[b, :, ROWS - 1 - far, :]
                z_out[base + 2 * b + far] = jnp.where(upper, top, bottom)
                r_out[base + 2 * b + far] = jnp.where(upper, bottom, top)
    _, corner = packed(tracers, rates_out, [lambda b: z_out[base + 2 * b]])
    for xz_out in xz_outs:
        xz_out[share + 1] = corner[0]


def pack_kernel(n, rates, c, r, sums, edges, *outs):
    tracers = c.shape[0]
    _, lon, _ = position()
    base = LEVELS + n
    tiles = [lambda b, k=k: c[b, k] for k in range(LEVELS)] + [lambda b: r[base + 2 * b]]
    total, edge = packed(tracers, rates, tiles)
    for k in range(LEVELS):
        sums[k], edges[k] = total[k], edge[k]
    low = iota((ROWS, LANES), 1) % 4 < 2
    share = LEVELS // n

    for s, out in enumerate(outs):
        m = lax.rem(lon + (s + 1), n)
        to_east = m > lon
        for level in range(share):
            out[LEVELS // 2 + 1 + level] = r[level * n + m]
        e, w = lax.rem(m + 1, n), lax.rem(m + n - 1, n)
        out[LEVELS // 2 + 1 + share] = sides_of(lambda level, block: r[level * n + block], share, e, w)
        for i in range(LEVELS // 2):
            a, b = (jnp.where(to_east, q, roll(q, -2, 1)) for q in (edge[2 * i], edge[2 * i + 1]))
            out[i] = jnp.where(low, a, roll(b, 2, 1))
        out[LEVELS // 2] = edge[LEVELS]


def split(q):
    high = q.astype(jnp.bfloat16)
    return high, (q - high.astype(jnp.float32)).astype(jnp.bfloat16)


def spread_kernel(rates, m_all, e_all):
    tracers = rates.shape[0]
    exact = functools.partial(jnp.dot, precision=lax.Precision.HIGHEST, preferred_element_type=jnp.float32)
    for group, transposed, size, out in ((ROWS, False, m_all.shape[0], m_all), (4, True, e_all.shape[1], e_all)):
        rows = (iota((size, tracers), 0) // group == iota((size, tracers), 1)).astype(jnp.float32)
        cols = (iota((tracers, size), 1) // group == iota((tracers, size), 0)).astype(jnp.float32)
        wide = exact(exact(rows, rates[...].T if transposed else rates[...]), cols)
        same = iota((size, size), 0) % group == iota((size, size), 1) % group
        high, low = split(jnp.where(same, wide, 0.0))
        out[...] = jnp.concatenate([high, high, low], axis=0 if transposed else 1)


def stacked(q, axis):
    high, low = split(q)
    return jnp.concatenate([high, low, high], axis=axis)


def product(left, right):
    return jnp.dot(left, right, preferred_element_type=jnp.float32)


class Halo:
    def __init__(self, pos, strips):
        self.upper = pos[2] == 1
        end = jnp.logical_or(
            jnp.logical_and(pos[0] == 0, jnp.logical_not(self.upper)),
            jnp.logical_and(pos[0] == strips - 1, self.upper),
        )
        self.keep_z = jnp.where(end, 0.0, 1.0)
        self.from_r = (iota((ROWS, LANES), 0) >= ROWS // 2) == self.upper

    def rows(self, r, z):
        return jnp.where(self.from_r, r, z * self.keep_z)

    def sides(self, r, z):
        z = z * self.keep_z
        return jnp.where(self.upper, r, z), jnp.where(self.upper, z, r)


def flow_kernel(n, strips, *refs):
    rates, f, count, c, sums, m_all, e_all, z, r = refs[:9]
    del m_all, e_all
    pos = position()
    others = n - 1
    xs, xzs, x2s = (refs[9 + i * others : 9 + (i + 1) * others] for i in range(3))
    coef1, coef2, ends, rims, f_out = refs[9 + 3 * others : 14 + 3 * others]
    heats = refs[14 + 3 * others : 14 + 4 * others]
    dyn, mix, depth, all_edges, all_rims, out, light_out = refs[14 + 4 * others :]
    tracers, share = c.shape[0], f.shape[1]
    strip, lon = pos[0], pos[1]
    halo = Halo(pos, strips)
    lane = iota((ROWS, LANES), 1)
    first, second = slice(0, LANES), slice(LANES, RING_COLS)
    own_rows, far_rows = slice(0, ROWS), slice(ROWS, RING_ROWS)
    base = LEVELS + n
    half = ROWS // 2

    def beside(m):
        return lax.rem(m + 1, n), lax.rem(m + n - 1, n)

    def window(main, near, m):
        east, west = beside(m)

        def side(g):
            return g(east) if n == 2 else jnp.where(lane < LANES // 2, g(east), g(west))

        return main(m), side(main), near(m), side(near)

    def put(ref, at, tiles):
        for tile, (rows, cols) in zip(
            tiles, ((own_rows, first), (own_rows, second), (far_rows, first), (far_rows, second))
        ):
            ref[(*at, rows, cols)] = tile

    def own_window(field, level, m):
        def near(block):
            return next_rows(*halo.sides(r[level * n + block], z[level * n + block]), field)

        return window(lambda block: f[field, level, :, block_of(block)], near, m)

    for field in range(FIELDS):
        for level in range(share):
            put(dyn, (field, lon * share + level), own_window(field, level, lon))

    def depth_window(m):
        return window(
            lambda block: count[:, block_of(block)].astype(jnp.float32),
            lambda block: halo.rows(r[LEVELS + block], z[LEVELS + block]),
            m,
        )

    put(depth, (), depth_window(lon))

    sides = FIELDS * share
    low = LEVELS // 2 + 1
    for s, (x, xz, x2) in enumerate(zip(xs, xzs, x2s)):
        m = lax.rem(lon + (n - 1 - s), n)
        for level in range(share):
            shift = -(2 * NEAR * level + NEAR)
            near = halo.sides(x2[low + level], xz[level])
            corners = halo.sides(roll(x2[low + share], shift, 1), roll(xz[share], shift, 1))
            for field in range(FIELDS):
                i = field * share + level
                put(
                    dyn,
                    (field, m * share + level),
                    (
                        x[i],
                        roll(x[sides], -(2 * NEAR * i + NEAR), 1),
                        next_rows(*near, field),
                        next_rows(*corners, field),
                    ),
                )
        all_edges[m] = x2[: LEVELS // 2]
        all_rims[m, 0], all_rims[m, 1] = halo.sides(x2[low - 1], xz[share + 1])

    east, west = beside(lon)
    easterly = lane % 4 >= 2
    exists = jnp.where(easterly, jnp.where(lon < n - 1, 1.0, 0.0), jnp.where(lon > 0, 1.0, 0.0))
    for k in range(LEVELS):
        e, w = all_edges[east, k // 2], all_edges[west, k // 2]
        if k % 2:
            w = roll(w, -2, 1)
        else:
            e = roll(e, 2, 1)
        ends[k] = jnp.where(easterly, e, w) * exists
    for side in range(2):
        rims[side] = jnp.where(easterly, all_rims[east, side], all_rims[west, side]) * exists

    mix[0, :, own_rows, first] = c[0]
    mix[1, :, own_rows, first] = sums[...]
    for i, b in enumerate((0, tracers)):
        for k in range(LEVELS):
            mix[i, k, own_rows, second] = roll(ends[k], -(4 * b + 2), 1)
        for side, place in enumerate((RING_ROWS - 1, ROWS)):
            mix[i, :, place, second] = roll(rims[side], -(4 * b + 2), 1)
    for far in range(2):
        total = [jnp.zeros((LEVELS, LANES), jnp.float32)] * 2
        for b in range(tracers):
            rows = halo.sides(r[base + 2 * b + far], z[base + 2 * b + far])
            if b == 0:
                chl = rows
            rate = jnp.broadcast_to(rates[:1, b : b + 1], (ROWS, LANES))
            total = [a + rate * q for a, q in zip(total, rows)]
        for i, rows in enumerate((chl, total)):
            mix[i, :, RING_ROWS - 1 - far, first] = rows[0]
            mix[i, :, ROWS + far, first] = rows[1]

    wide = (RING_ROWS, RING_COLS)
    ring_row, ring_col = iota(wide, 0), iota(wide, 1)
    row = strip * ROWS + jnp.where(ring_row < ROWS + half, ring_row, ring_row - RING_ROWS)
    fcor = 2.0 * (row.astype(jnp.float32) + 0.5) / (strips * ROWS) - 1.0

    def north(q):
        return roll(q, -1, 0)

    def south(q):
        return roll(q, 1, 0)

    def around(m):
        e, w = beside(m)
        block = jnp.where(ring_col < LANES, m, jnp.where(ring_col < LANES + LANES // 2, e, w))
        col = block * LANES + ring_col % LANES
        not_last, not_first = col < n * LANES - 1, col > 0
        return (
            lambda q: jnp.where(not_last, roll(q, -1, 1), 0.0),
            lambda q: jnp.where(not_first, roll(q, 1, 1), 0.0),
        )

    def masks(k, counts, east):
        wet = jnp.where(counts > k.astype(jnp.float32), 1.0, 0.0)
        return wet, wet * east(wet), wet * north(wet)

    def advance(uu, vv, tt, wets, east, west):
        wet, wet_u, wet_v = wets

        def lap(q, e, nn):
            return e + west(q) + nn + south(q) - 4.0 * q

        te, tn = east(tt), north(tt)
        u_new = wet_u * (uu + 0.1 * lap(uu, east(uu), north(uu)) + 0.3 * fcor * vv - 0.2 * (te - tt))
        v_new = wet_v * (vv + 0.1 * lap(vv, east(vv), north(vv)) - 0.3 * fcor * uu - 0.2 * (tn - tt))
        return u_new, v_new, wet * (tt + 0.1 * lap(tt, te, tn))

    def coefficients(uu, vv, uw, vs):
        a0 = 1.0 - 0.5 * (
            (jnp.maximum(uu, 0.0) - jnp.minimum(uw, 0.0)) + (jnp.maximum(vv, 0.0) - jnp.minimum(vs, 0.0))
        )
        return (
            a0,
            -0.5 * jnp.minimum(uu, 0.0),
            0.5 * jnp.maximum(uw, 0.0),
            -0.5 * jnp.minimum(vv, 0.0),
            0.5 * jnp.maximum(vs, 0.0),
        )

    east_of, west_of = around(lon)

    def one_level(k, carry):
        tau1, top1, tau2, top2 = carry
        wets = masks(k, depth[...], east_of)
        wet = wets[0]
        heat0 = dyn[3, k]
        uu, vv, tt = advance(dyn[0, k], dyn[1, k], dyn[2, k], wets, east_of, west_of)
        tt = tt + 0.5 * (wet * heat0)
        stencil = coefficients(uu, vv, west_of(uu), south(vv))

        def advect(q):
            a0, ae, aw, an, a_s = stencil
            return a0 * q + (ae * east_of(q) + aw * west_of(q)) + (an * north(q) + a_s * south(q))

        moved = advect(mix[0, k])
        tau1 = tau1 + (0.1 + 0.3 * jnp.maximum(moved, 0.0))
        below = jnp.exp(-tau1)
        half_wet = 0.5 * wet
        warm = half_wet * (2.0 * (top1 - below))
        light = half_wet * top1
        for i, q in enumerate((*stencil, wet, light)):
            coef1[i, k] = q
        chl = wet * moved + light * advect(mix[1, k])
        top1 = below

        uu, vv, tt = advance(uu, vv, tt, wets, east_of, west_of)
        inner = (own_rows, first)
        own = [q[inner] for q in coefficients(uu, vv, west_of(uu), south(vv))]
        moved = (
            own[0] * chl[inner]
            + (own[1] * east_of(chl)[inner] + own[2] * west_of(chl)[inner])
            + (own[3] * north(chl)[inner] + own[4] * south(chl)[inner])
        )
        tau2 = tau2 + (0.1 + 0.3 * jnp.maximum(moved, 0.0))
        below = jnp.exp(-tau2)
        for i, q in enumerate((*own, wet[inner], half_wet[inner] * top2)):
            coef2[i, k] = q
        light_out[0, k] = warm[inner]
        light_out[1, k] = 2.0 * wet[inner] * (top2 - below)
        out[0, k], out[1, k], out[2, k] = uu[own_rows], vv[own_rows], tt[own_rows]
        return tau1, top1, tau2, below

    big = jnp.zeros(wide, jnp.float32)
    small = jnp.zeros((ROWS, LANES), jnp.float32)
    lax.fori_loop(0, LEVELS, one_level, (big, big + 1.0, small, small + 1.0), unroll=2)

    here = block_of(lon)
    for level in range(share):
        k = lon * share + level
        for i in range(3):
            q = out[i, k, :, first]
            f_out[i, level, :, here] = q + light_out[0, k] if i == 2 else q
            if n == 2:
                f_out[i, level, :, block_of(1 - lon)] = out[i, k, :, second]
        f_out[3, level, :, here] = light_out[1, k]
    for s, heat in enumerate(heats):
        m = lax.rem(lon + (s + 1), n)
        for i in range(2):
            heat[i] = light_out[i, pl.ds(m * share, share)]

    if n > 2:

        def other_block(s, carry):
            m = lax.rem(lon + s, n)
            e, w = around(m)
            put(depth, (), depth_window(m))
            for level in range(share):
                k = lon * share + level
                wets = masks(k, depth[...], e)
                for field in range(FIELDS):
                    put(dyn, (field, k), own_window(field, level, m))
                uu, vv, tt = advance(dyn[0, k], dyn[1, k], dyn[2, k], wets, e, w)
                tt = tt + 0.5 * (wets[0] * dyn[3, k])
                for i, q in enumerate(advance(uu, vv, tt, wets, e, w)):
                    f_out[i, level, :, block_of(m)] = q[own_rows, first]
            return carry

        lax.fori_loop(1, n, other_block, 0)


def tile_stencil(q, rim, columns, stencil, sub, lane):
    a0, ae, aw, an, a_s = stencil
    e = jnp.where(lane == LANES - 1, columns, roll(q, -1, 1))
    w = jnp.where(lane == 0, columns, roll(q, 1, 1))
    up = jnp.where(sub == ROWS - 1, rim, roll(q, -1, 0))
    down = jnp.where(sub == 0, rim, roll(q, 1, 0))
    return a0 * q + (ae * e + aw * w) + (an * up + a_s * down)


def swapped(q):
    return jnp.where(iota(q.shape, 1) % 4 == 1, roll(q, -1, 1), roll(q, 1, 1))


def beside_columns(edge, b):
    return roll(edge, LANES - 2 - 4 * b, 1)


def part_of(b, half):
    return slice(b * ROWS, (b + 1) * ROWS), slice(half * LANES, (half + 1) * LANES)


def tile_loop(pairs, source, rims, edge, coef, m_all, adv, store):
    tracers = source.shape[0]
    sub, lane = iota((ROWS, LANES), 0), iota((ROWS, LANES), 1)
    for i in pairs:
        for half in range(2):
            k = 2 * i + half
            stencil = [coef(j, k) for j in range(5)]
            columns = edge[k]
            for b in range(tracers):
                adv[(i, *part_of(b, half))] = tile_stencil(
                    source[b, k], rims[b, k], beside_columns(columns, b), stencil, sub, lane
                )
        react = product(m_all[...], stacked(adv[i], 0))
        for half in range(2):
            k = 2 * i + half
            wet, light = coef(5, k), coef(6, k)
            for b in range(tracers):
                store(b, k, wet * adv[(i, *part_of(b, half))] + light * react[part_of(b, half)])
        yield i


def tracer_kernel(
    n, strips, c, edges, ends, rims, coef, coef2, m_all, e_all, z, r, done, c_out, row1, edge1, row0, edge0, adv, adv2
):
    pos = position()
    tracers = c.shape[0]
    lon = pos[1]
    halo = Halo(pos, strips)
    sub, lane = iota((ROWS, LANES), 0), iota((ROWS, LANES), 1)
    easterly = lane % 4 >= 2
    base = LEVELS + n

    rim = row0.at[0]
    rim[:, 0, :] = rims[0]
    rim[:, ROWS - 1, :] = rims[1]
    parts = []
    for k in range(LEVELS):
        q, inside = ends[k], edges[k]
        outer = jnp.where(easterly, roll(q, -1, 1), roll(q, 1, 1))
        inner = jnp.where(easterly, roll(inside, 1, 1), roll(inside, -1, 1))
        up = jnp.where(sub == ROWS - 1, rim[k], roll(q, -1, 0))
        down = jnp.where(sub == 0, rim[k], roll(q, 1, 0))

        def at_edge(i):
            side = coef[i, k, :ROWS, LANES:]
            return (
                jnp.broadcast_to(side[:, :1], (ROWS, LANES)),
                jnp.broadcast_to(side[:, LANES - 1 :], (ROWS, LANES)),
            )

        def pick(pair):
            return jnp.where(easterly, pair[0], pair[1])

        a0, ae, aw, an, a_s, wet, light = (at_edge(i) for i in range(7))
        moved = (
            pick(a0) * q
            + (pick((ae[0], aw[1])) * outer + pick((aw[0], ae[1])) * inner)
            + (pick(an) * up + pick(a_s) * down)
        )
        parts.append((moved, pick(wet), pick(light)))
        edge0[k] = swapped(q)
    react = product(stacked(jnp.concatenate([p[0] for p in parts], axis=0), 1), e_all[...])
    east_exists = jnp.where(lon < n - 1, 1.0, 0.0)
    west_exists = jnp.where(lon > 0, 1.0, 0.0)
    exists = jnp.where(easterly, east_exists, west_exists)
    for k, (q, wet, light) in enumerate(parts):
        edge1[k] = swapped((wet * q + light * react[k * ROWS : (k + 1) * ROWS]) * exists)

    places = ((0, RING_ROWS - 1), (ROWS - 1, ROWS))
    corners = [swapped(rims[side]) for side in range(2)]
    stencils = [[coef[i, :, place, :LANES] for i in range(7)] for _, place in places]
    for b in range(tracers):
        near = halo.sides(r[base + 2 * b], z[base + 2 * b])
        far = halo.sides(r[base + 2 * b + 1], z[base + 2 * b + 1])
        for side, (at, _) in enumerate(places):
            a0, ae, aw, an, a_s, _, _ = stencils[side]
            q = near[side]
            row0[b, :, at, :] = q
            columns = beside_columns(corners[side], b)
            e = jnp.where(lane == LANES - 1, columns, roll(q, -1, 1))
            w = jnp.where(lane == 0, columns, roll(q, 1, 1))
            inner = c[b, :, at, :]
            up, down = (inner, far[side]) if side == 0 else (far[side], inner)
            adv[(LEVELS // 2, *part_of(b, side))] = a0 * q + (ae * e + aw * w) + (an * up + a_s * down)
    react = product(m_all[...], stacked(adv[LEVELS // 2], 0))
    for b in range(tracers):
        for side, (at, _) in enumerate(places):
            wet, light = stencils[side][5:]
            row1[b, :, at, :] = wet * adv[(LEVELS // 2, *part_of(b, side))] + light * react[part_of(b, side)]

    def store(b, k, q):
        c_out[b, k] = q

    def store_done(b, k, q):
        done[b, k] = q

    pairs = range(LEVELS // 2)
    for _ in tile_loop(pairs, c, row0, edge0, lambda i, k: coef[i, k, :ROWS, :LANES], m_all, adv, store):
        pass
    pairs = range(done.shape[1] // 2)
    for _ in tile_loop(pairs, c_out, row1, edge1, lambda i, k: coef2[i, k], m_all, adv2, store_done):
        pass


def last_kernel(n, *refs):
    others = n - 1
    c, f = refs[:2]
    heats = refs[2 : 2 + others]
    u_out, v_out, t_out, h_out, c_out = refs[2 + others : 7 + others]
    warm, sem, c_sem = refs[7 + others :]
    share = f.shape[1]
    _, lon, _ = position()
    batch = c.shape[0] // c_sem.shape[0]
    copies = []
    for i in range(c_sem.shape[0]):
        part = pl.ds(i * batch, batch)
        copies.append(pltpu.make_async_copy(c.at[part], c_out.at[part], c_sem.at[i]))
    copies += [pltpu.make_async_copy(f.at[i], ref, sem.at[i]) for i, ref in enumerate((u_out, v_out))]
    for copy in copies:
        copy.start()
    here = block_of(lon)
    for level in range(share):
        warm[0, level, :, here] = f[2, level, :, here]
        warm[1, level, :, here] = f[3, level, :, here]
        for s, heat in enumerate(heats):
            there = block_of(lax.rem(lon + (n - 1 - s), n))
            warm[0, level, :, there] = f[2, level, :, there] + heat[0, level]
            warm[1, level, :, there] = heat[1, level]
    copies += [pltpu.make_async_copy(warm.at[i], ref, sem.at[2 + i]) for i, ref in enumerate((t_out, h_out))]
    for copy in copies[-2:]:
        copy.start()
    for copy in copies:
        copy.wait()


def shards(groups, n, lats, u, v, t, h, c, count, rates):
    tracers = c.shape[0]
    share, width = u.shape[0], u.shape[2]
    strips = lats * CORES
    vmem = pl.BlockSpec(memory_space=pltpu.VMEM)
    anywhere = pl.BlockSpec(memory_space=pl.ANY)
    hbm = pl.BlockSpec(memory_space=pltpu.HBM)
    params = pltpu.CompilerParams(vmem_limit_bytes=32 * 1024 * 1024)
    dma = pltpu.SemaphoreType.DMA

    def shape(*dims, dtype=jnp.float32):
        return jax.ShapeDtypeStruct(dims, dtype)

    def tiles(*dims):
        return shape(*dims, ROWS, LANES)

    def scratch(*dims):
        return pltpu.VMEM(dims, jnp.float32)

    def call(kernel, name, args, in_specs, out_shape, out_specs=None, scratch_shapes=()):
        return pl.pallas_call(
            kernel,
            out_shape=tuple(out_shape),
            in_specs=in_specs,
            out_specs=out_specs or (vmem,) * len(out_shape),
            scratch_shapes=scratch_shapes,
            compiler_params=params,
            name=name,
        )(*args)

    def permute(q, target):
        pairs = []
        for g in range(groups):
            for a in range(lats):
                for o in range(n):
                    for i in range(CORES):
                        g2, a2, o2, i2 = target(g, a, o, i)
                        pairs.append(
                            (((g * lats + a) * n + o) * CORES + i, ((g2 * lats + a2) * n + o2) * CORES + i2)
                        )
        return lax.ppermute(q, ("grp", "lat", "lon", "role"), pairs)

    def z_target(shift):
        def target(g, a, o, i):
            s = a * CORES + i + (1 if i else -1)
            if 0 <= s < strips:
                return g, s // CORES, (o + shift) % n, s % CORES
            return (g ^ 1 if g ^ 1 < groups else g), a, o, i

        return target

    def x_target(shift):
        return lambda g, a, o, i: (g, a, (o + shift) % n, i)

    def r_target(g, a, o, i):
        return g, a, o, 1 - i

    shifts = range(1, n)
    z_tiles = LEVELS + n + 2 * tracers
    x_tiles = FIELDS * share + 1
    xz_tiles = share + 2
    f, c_here, depth, rates, z_pay, r_pay, *pays = call(
        functools.partial(load_kernel, n),
        "load",
        [pltpu.with_memory_space_constraint(q, pltpu.HBM) for q in (u, v, t, h, count, rates, c)],
        [hbm] * 7,
        [
            shape(FIELDS, *u.shape),
            shape(*c.shape),
            shape(*count.shape, dtype=jnp.int32),
            shape(*rates.shape),
            tiles(z_tiles),
            tiles(z_tiles),
        ]
        + [tiles(x_tiles)] * (n - 1)
        + [tiles(xz_tiles)] * (n - 1),
        scratch_shapes=[dma((FIELDS + 2,)), dma((4,))],
    )
    r_in = permute(r_pay, r_target)
    z_in = permute(z_pay, z_target(0))
    xs = [permute(q, x_target(s)) for s, q in zip(shifts, pays[: n - 1])]
    xzs = [permute(q, z_target(s)) for s, q in zip(shifts, pays[n - 1 :])]
    sums, edges, *pays = call(
        functools.partial(pack_kernel, n),
        "pack",
        (rates, c_here, r_in),
        [vmem] * 3,
        [tiles(LEVELS)] * 2 + [tiles(LEVELS // 2 + 2 + share)] * (n - 1),
    )
    x2s = [permute(q, x_target(s)) for s, q in zip(shifts, pays)]

    m_size, e_size = tracers * ROWS, LANES
    bf16 = jnp.bfloat16
    m_all, e_all = call(
        spread_kernel,
        "spread",
        (rates,),
        [vmem],
        [shape(m_size, 3 * m_size, dtype=bf16), shape(3 * e_size, e_size, dtype=bf16)],
    )

    args = (rates, f, depth, c_here, sums, m_all, e_all, z_in, r_in, *xs, *xzs, *x2s)
    coef1, coef2, ends, rims, f_new, *heats = call(
        functools.partial(flow_kernel, n, strips),
        "flow",
        args,
        [vmem] * len(args),
        [
            shape(7, LEVELS, RING_ROWS, RING_COLS),
            tiles(7, LEVELS),
            tiles(LEVELS),
            shape(2, LEVELS, LANES),
            shape(FIELDS, *u.shape),
        ]
        + [tiles(2, share)] * (n - 1),
        scratch_shapes=[
            scratch(FIELDS, LEVELS, RING_ROWS, RING_COLS),
            scratch(2, LEVELS, RING_ROWS, RING_COLS),
            scratch(RING_ROWS, RING_COLS),
            scratch(n, LEVELS // 2, ROWS, LANES),
            scratch(n, 2, LEVELS, LANES),
            scratch(3, LEVELS, ROWS, RING_COLS),
            scratch(2, LEVELS, ROWS, LANES),
        ],
    )
    heats = [permute(q, x_target(s)) for s, q in zip(shifts, heats)]
    args = (c_here, edges, ends, rims, coef1, coef2, m_all, e_all, z_in, r_in)
    (c_new,) = call(
        functools.partial(tracer_kernel, n, strips),
        "tracers",
        args,
        [vmem] * len(args),
        [shape(*c.shape)],
        scratch_shapes=[
            scratch(*c.shape),
            scratch(tracers, LEVELS, ROWS, LANES),
            scratch(LEVELS, ROWS, LANES),
            scratch(tracers, LEVELS, ROWS, LANES),
            scratch(LEVELS, ROWS, LANES),
            scratch(LEVELS // 2 + 1, tracers * ROWS, 2 * LANES),
            scratch(LEVELS // 2, tracers * ROWS, 2 * LANES),
        ],
    )
    args = (c_new, f_new, *heats)
    return call(
        functools.partial(last_kernel, n),
        "last",
        args,
        [vmem] * len(args),
        [shape(*u.shape)] * FIELDS + [shape(*c.shape)],
        out_specs=(anywhere,) * 5,
        scratch_shapes=[scratch(2, *u.shape), dma((FIELDS,)), dma((4,))],
    )


def solution(mesh):
    level = P("lon", ("grp", "lat", "role"), None)
    tracer = P(None, None, ("grp", "lat", "role"), "lon")
    return jax.shard_map(
        functools.partial(shards, mesh.shape["grp"], mesh.shape["lon"], mesh.shape["lat"]),
        mesh=mesh,
        in_specs=(level, level, level, level, tracer, P(("grp", "lat", "role"), None), P()),
        out_specs=(level, level, level, level, tracer),
        check_vma=False,
    )
```

```python
import functools

import jax
import jax.numpy as jnp
from jax import lax
from jax.experimental import pallas as pl
from jax.experimental.pallas import tpu as pltpu
from jax.sharding import PartitionSpec as P

ROWS = 8
LANES = 128
LEVELS = 8
CORES = 2
FIELDS = 4
NEAR = 3

RING_ROWS = 2 * ROWS
RING_COLS = 2 * LANES


def iota(shape, dim):
    return lax.broadcasted_iota(jnp.int32, shape, dim)


def roll(q, shift, axis):
    return pltpu.roll(q, shift % q.shape[axis], axis)


def position():
    lat, lon, role = lax.axis_index("lat"), lax.axis_index("lon"), lax.axis_index("role")
    return lat * CORES + role, lon, role


def block_of(m):
    return pl.ds(pl.multiple_of(m * LANES, LANES), LANES)


def packed(tracers, rates, tiles):
    lane = iota((ROWS, LANES), 1)
    zero = jnp.zeros((ROWS, LANES), jnp.float32)
    total, edge = [zero] * len(tiles), [zero] * len(tiles)
    for b in range(tracers):
        rate = jnp.broadcast_to(rates[:1, b : b + 1], (ROWS, LANES))
        mine = lane // 4 == b
        for i, get in enumerate(tiles):
            q = get(b)
            total[i] = total[i] + rate * q
            edge[i] = jnp.where(mine, roll(q, 4 * b + 2, 1), edge[i])
    mine = lane // 4 == tracers
    return total, [jnp.where(mine, roll(t, 4 * tracers + 2, 1), e) for t, e in zip(total, edge)]


def last_rows(tiles):
    u, v, t, h = tiles
    sub = iota((ROWS, LANES), 0)
    low = jnp.where(sub >= 1, roll(t, -5, 0), roll(h, 1, 0))
    return jnp.where(sub >= 5, v, jnp.where(sub >= 3, roll(u, -3, 0), low))


def first_rows(tiles):
    u, v, t, h = tiles
    sub = iota((ROWS, LANES), 0)
    high = jnp.where(sub <= 6, roll(t, 5, 0), roll(h, -1, 0))
    return jnp.where(sub <= 2, v, jnp.where(sub <= 4, roll(u, 3, 0), high))


def next_rows(south, north, field):
    shift = (3, 0, 5, -1)[field]
    if shift:
        south, north = roll(south, shift, 0), roll(north, -shift, 0)
    return jnp.where(iota((ROWS, LANES), 0) >= ROWS // 2, south, north)


def sides_of(get, amount, east, west, into, start):
    lane = iota((ROWS, LANES), 1)
    for i in range(amount):
        first = start + 2 * NEAR * i
        side = jnp.where(lane < LANES // 2, get(i, east), get(i, west))
        into = jnp.where((lane >= first) & (lane < first + 2 * NEAR), roll(side, first + NEAR, 1), into)
    return into


def side_in(tile, i, start):
    return roll(tile, -(start + 2 * NEAR * i + NEAR), 1)


def load_kernel(n, u, v, t, h, count, rates, c, f_out, c_out, d_out, rates_out, z_out, r_out, f_sem, c_sem):
    tracers, share = c.shape[0], f_out.shape[1]
    _, _, role = position()
    upper = role == 1
    copies = [pltpu.make_async_copy(ref, f_out.at[i], f_sem.at[i]) for i, ref in enumerate((u, v, t, h))]
    copies.append(pltpu.make_async_copy(count, d_out, f_sem.at[FIELDS]))
    copies.append(pltpu.make_async_copy(rates, rates_out, f_sem.at[FIELDS + 1]))
    batch = tracers // c_sem.shape[0]
    c_copies = []
    for i in range(c_sem.shape[0]):
        part = pl.ds(i * batch, batch)
        c_copies.append(pltpu.make_async_copy(c.at[part], c_out.at[part], c_sem.at[i]))
    for copy in copies + c_copies:
        copy.start()
    for copy in copies:
        copy.wait()

    def whole(i, block):
        return f_out[i // share, i % share, :, block_of(block)]

    def strips_of(level, block):
        tiles = [whole(field * share + level, block) for field in range(FIELDS)]
        top, bottom = last_rows(tiles), first_rows(tiles)
        return jnp.where(upper, top, bottom), jnp.where(upper, bottom, top)

    count_f = FIELDS * share
    for level in range(share):
        for block in range(n):
            z_out[level * n + block], r_out[level * n + block] = strips_of(level, block)
    base = LEVELS
    for block in range(n):
        depth = d_out[:, block * LANES : (block + 1) * LANES].astype(jnp.float32)
        z_out[base + block] = depth
        r_out[base + block] = depth
    base += n
    for i, copy in enumerate(c_copies):
        copy.wait()
        for b in range(i * batch, (i + 1) * batch):
            for far in range(2):
                bottom, top = c_out[b, :, far, :], c_out[b, :, ROWS - 1 - far, :]
                z_out[base + 2 * b + far] = jnp.where(upper, top, bottom)
                r_out[base + 2 * b + far] = jnp.where(upper, bottom, top)


def edge_kernel(n, rates, c, sums, edges, *outs):
    _, lon, _ = position()
    total, edge = packed(c.shape[0], rates, [lambda b, k=k: c[b, k] for k in range(LEVELS)])
    for k in range(LEVELS):
        sums[k], edges[k] = total[k], edge[k]
    low = iota((ROWS, LANES), 1) % 4 < 2
    for s, out in enumerate(outs):
        to_east = lax.rem(lon + (s + 1), n) > lon
        for i in range(LEVELS // 2):
            a, b = (jnp.where(to_east, q, roll(q, -2, 1)) for q in (edge[2 * i], edge[2 * i + 1]))
            out[i] = jnp.where(low, a, roll(b, 2, 1))


def join_kernel(n, rates, f, z, r, *refs):
    pays, x_outs, xz_outs = (refs[i * (n - 1) : (i + 1) * (n - 1)] for i in range(3))
    _, lon, _ = position()
    tracers, share, base = rates.shape[0], LEVELS // n, LEVELS + n
    _, (rim_r, rim_z) = packed(tracers, rates, [lambda b: r[base + 2 * b], lambda b: z[base + 2 * b]])
    zero = jnp.zeros((ROWS, LANES), jnp.float32)
    count = FIELDS * share

    def whole(i, block):
        return f[i // share, i % share, :, block_of(block)]

    for s, (pay, x, xz) in enumerate(zip(pays, x_outs, xz_outs)):
        m = lax.rem(lon + (s + 1), n)
        e, w = lax.rem(m + 1, n), lax.rem(m + n - 1, n)
        for i in range(count):
            x[i] = whole(i, m)
        x[count : count + LEVELS // 2] = pay[...]
        end = count + LEVELS // 2
        for level in range(share):
            x[end + level] = r[level * n + m]
            xz[level] = z[level * n + m]
        x[end + share] = rim_r
        sides = sides_of(whole, count, e, w, zero, 0)
        x[end + share + 1] = sides_of(
            lambda level, block: r[level * n + block], share, e, w, sides, 2 * NEAR * count
        )
        xz[share] = sides_of(lambda level, block: z[level * n + block], share, e, w, rim_z, 4 * (tracers + 1))


def split(q):
    high = q.astype(jnp.bfloat16)
    return high, (q - high.astype(jnp.float32)).astype(jnp.bfloat16)


def spread_kernel(rates, m_all, e_all):
    tracers = rates.shape[0]
    for group, transposed, size, out in ((ROWS, False, m_all.shape[0], m_all), (4, True, e_all.shape[1], e_all)):
        rows = (iota((size, tracers), 0) // group == iota((size, tracers), 1)).astype(jnp.bfloat16)
        cols = (iota((tracers, size), 1) // group == iota((tracers, size), 0)).astype(jnp.bfloat16)
        same = iota((size, size), 0) % group == iota((size, size), 1) % group
        parts = []
        for q in split(rates[...].T if transposed else rates[...]):
            wide = product(product(rows, q).astype(jnp.bfloat16), cols)
            parts.append(jnp.where(same, wide, 0.0).astype(jnp.bfloat16))
        high, low = parts
        out[...] = jnp.concatenate([high, high, low], axis=0 if transposed else 1)


def stacked(q, axis):
    high, low = split(q)
    return jnp.concatenate([high, low, high], axis=axis)


def product(left, right):
    return jnp.dot(left, right, preferred_element_type=jnp.float32)


def advected(q, e, w, up, down, stencil):
    a0, mu, pw, mv, ps = stencil
    return (a0 * q + (pw * w - mu * e)) + (ps * down - mv * up)


class Halo:
    def __init__(self, pos, strips):
        self.upper = pos[2] == 1
        end = jnp.logical_or(
            jnp.logical_and(pos[0] == 0, jnp.logical_not(self.upper)),
            jnp.logical_and(pos[0] == strips - 1, self.upper),
        )
        self.keep_z = jnp.where(end, 0.0, 1.0)
        self.from_r = (iota((ROWS, LANES), 0) >= ROWS // 2) == self.upper

    def rows(self, r, z):
        return jnp.where(self.from_r, r, z * self.keep_z)

    def sides(self, r, z):
        z = z * self.keep_z
        return jnp.where(self.upper, r, z), jnp.where(self.upper, z, r)


FIRST, SECOND = slice(0, LANES), slice(LANES, RING_COLS)
OWN_ROWS, FAR_ROWS = slice(0, ROWS), slice(ROWS, RING_ROWS)
WIDE = (RING_ROWS, RING_COLS)


def put(ref, at, tiles):
    places = ((OWN_ROWS, FIRST), (OWN_ROWS, SECOND), (FAR_ROWS, FIRST), (FAR_ROWS, SECOND))
    for tile, (rows, cols) in zip(tiles, places):
        ref[(*at, rows, cols)] = tile


def beside(m, n):
    return lax.rem(m + 1, n), lax.rem(m + n - 1, n)


def north(q):
    return roll(q, -1, 0)


def south(q):
    return roll(q, 1, 0)


def east(q):
    return roll(q, -1, 1)


def west(q):
    return roll(q, 1, 1)


def around(m, n):
    e, w = beside(m, n)
    ring_col = iota(WIDE, 1)
    block = jnp.where(ring_col < LANES, m, jnp.where(ring_col < LANES + LANES // 2, e, w))
    col = block * LANES + ring_col % LANES
    not_last, not_first = col < n * LANES - 1, col > 0
    return lambda q: jnp.where(not_last, east(q), 0.0), lambda q: jnp.where(not_first, west(q), 0.0)


def coriolis(strip, strips):
    ring_row = iota(WIDE, 0)
    row = strip * ROWS + jnp.where(ring_row < ROWS + ROWS // 2, ring_row, ring_row - RING_ROWS)
    return 0.3 * (2.0 * (row.astype(jnp.float32) + 0.5) / (strips * ROWS) - 1.0)


def masks(k, counts, east_of):
    wet = jnp.where(counts > k, 1.0, 0.0)
    return wet, wet * east_of(wet), wet * north(wet)


def advance(uu, vv, tt, wet_u, wet_v, turn, east_of, west_of, again):
    def mixed(q, e, w, nn):
        return 0.6 * q + 0.1 * ((e + w) + (nn + south(q)))

    te, tn = east_of(tt), north(tt)
    u_west = west(uu) if again else west_of(uu)
    u_new = wet_u * (mixed(uu, east(uu), u_west, north(uu)) + (turn * vv - 0.2 * (te - tt)))
    v_new = wet_v * (mixed(vv, east_of(vv), west_of(vv), north(vv)) - (turn * uu + 0.2 * (tn - tt)))
    return u_new, v_new, mixed(tt, te, west_of(tt), tn)


def coefficients(uu, vv):
    uu, vv = 0.5 * uu, 0.5 * vv
    uw, vs = west(uu), south(vv)
    pw, ps = jnp.maximum(uw, 0.0), jnp.maximum(vs, 0.0)
    mu, mv = jnp.minimum(uu, 0.0), jnp.minimum(vv, 0.0)
    a0 = (1.0 - (jnp.maximum(uu, 0.0) - jnp.minimum(uw, 0.0))) - (jnp.maximum(vv, 0.0) - jnp.minimum(vs, 0.0))
    return a0, mu, pw, mv, ps


def two_steps(read, wets, turn, shifts):
    uu, vv, tt = advance(read(0), read(1), read(2), *wets[1:], turn, *shifts, False)
    tt = wets[0] * (tt + 0.5 * read(3))
    stencil = coefficients(uu, vv)
    uu, vv, tt = advance(uu, vv, tt, *wets[1:], turn, *shifts, True)
    return uu, vv, wets[0] * tt, stencil, [q[OWN_ROWS, FIRST] for q in coefficients(uu, vv)]


def own_kernel(n, strips, rates, f, count, c, sums, z, r, coef1, coef2, wets, mix, f_out, dyn, depth):
    tracers, share = c.shape[0], f.shape[1]
    strip, lon, _ = pos = position()
    halo = Halo(pos, strips)
    lane = iota((ROWS, LANES), 1)
    base = LEVELS + n

    def window(main, near, m):
        e, w = beside(m, n)

        def side(g):
            return g(e) if n == 2 else jnp.where(lane < LANES // 2, g(e), g(w))

        return main(m), side(main), near(m), side(near)

    def own_window(field, level, m):
        def near(block):
            return next_rows(*halo.sides(r[level * n + block], z[level * n + block]), field)

        return window(lambda block: f[field, level, :, block_of(block)], near, m)

    def depth_window(m):
        return window(
            lambda block: count[:, block_of(block)].astype(jnp.float32),
            lambda block: halo.rows(r[LEVELS + block], z[LEVELS + block]),
            m,
        )

    put(depth, (), depth_window(lon))
    for field in range(FIELDS):
        for level in range(share):
            put(dyn, (field, level), own_window(field, level, lon))
    turn = coriolis(strip, strips)
    shifts = around(lon, n)
    for k in range(LEVELS):
        for i, q in enumerate(masks(float(k), depth[...], shifts[0])):
            wets[i, k] = q

    def one_level(level, carry):
        wet = [wets[i, lon * share + level] for i in range(3)]
        uu, vv, tt, stencil, stencil2 = two_steps(lambda i: dyn[i, level], wet, turn, shifts)
        for i, q in enumerate(stencil):
            coef1[i, level] = q
        for i, q in enumerate(stencil2):
            coef2[i, level] = q
        for i, q in enumerate((uu, vv, tt)):
            f_out[i, level, :, block_of(lon)] = q[OWN_ROWS, FIRST]
            if n == 2:
                f_out[i, level, :, block_of(1 - lon)] = q[OWN_ROWS, SECOND]
        return carry

    lax.fori_loop(0, share, one_level, 0, unroll=min(2, share))

    mix[0, :, OWN_ROWS] = c[0]
    mix[1, :, OWN_ROWS] = sums[...]
    for far in range(2):
        total = [jnp.zeros((LEVELS, LANES), jnp.float32)] * 2
        for b in range(tracers):
            rows = halo.sides(r[base + 2 * b + far], z[base + 2 * b + far])
            if b == 0:
                chl = rows
            rate = jnp.broadcast_to(rates[:1, b : b + 1], (ROWS, LANES))
            total = [a + rate * q for a, q in zip(total, rows)]
        for i, rows in enumerate((chl, total)):
            mix[i, :, RING_ROWS - 1 - far] = rows[0]
            mix[i, :, ROWS + far] = rows[1]

    if n > 2:

        def other_block(s, carry):
            m = lax.rem(lon + s, n)
            around_m = around(m, n)
            put(depth, (), depth_window(m))
            for level in range(share):
                k = (lon * share + level).astype(jnp.float32)
                for field in range(FIELDS):
                    put(dyn, (field, level), own_window(field, level, m))
                wet = masks(k, depth[...], around_m[0])
                after = two_steps(lambda i, level=level: dyn[i, level], wet, turn, around_m)
                for i, q in enumerate(after[:3]):
                    f_out[i, level, :, block_of(m)] = q[OWN_ROWS, FIRST]
            return carry

        lax.fori_loop(1, n, other_block, 0)


def flow_kernel(n, strips, tracers, *refs):
    own1, own2, wets, mix = refs[:4]
    others = n - 1
    xs, xzs = (refs[6 + i * others : 6 + (i + 1) * others] for i in range(2))
    coef1, coef2, ends, rims, light_out = refs[6 + 2 * others : 11 + 2 * others]
    heats = refs[11 + 2 * others : 11 + 3 * others]
    dyn, side_mix, all_edges, all_rims, moved = refs[11 + 3 * others :]
    share = own1.shape[1]
    strip, lon, _ = pos = position()
    halo = Halo(pos, strips)
    lane = iota((ROWS, LANES), 1)
    turn = coriolis(strip, strips)
    shifts = around(lon, n)
    mine = pl.ds(lon * share, share)
    for i in range(5):
        coef1[i, mine] = own1[i]
        coef2[i, mine] = own2[i]

    fields = FIELDS * share
    end = fields + LEVELS // 2
    last_lane = 4 * (tracers + 1)
    for s, (x, xz) in enumerate(zip(xs, xzs)):
        m = lax.rem(lon + (n - 1 - s), n)
        sides, far_sides = x[end + share + 1], xz[share]
        for level in range(share):
            near = halo.sides(x[end + level], xz[level])
            corners = halo.sides(side_in(sides, level, 2 * NEAR * fields), side_in(far_sides, level, last_lane))
            for field in range(FIELDS):
                i = field * share + level
                put(
                    dyn,
                    (field, s * share + level),
                    (x[i], side_in(sides, i, 0), next_rows(*near, field), next_rows(*corners, field)),
                )
        all_edges[m] = x[fields:end]
        all_rims[m, 0], all_rims[m, 1] = halo.sides(x[end + share], far_sides)

    def other_level(i):
        s, level = i // share, i % share
        k = lax.rem(lon + (n - 1 - s), n) * share + level
        wet = [wets[j, k] for j in range(3)]
        _, _, _, stencil, stencil2 = two_steps(lambda j: dyn[j, i], wet, turn, shifts)
        for j, q in enumerate(stencil):
            coef1[j, k] = q
        for j, q in enumerate(stencil2):
            coef2[j, k] = q

    for i in range(others * share):
        other_level(i)

    east_m, west_m = beside(lon, n)
    easterly = lane % 4 >= 2
    exists = jnp.where(easterly, jnp.where(lon < n - 1, 1.0, 0.0), jnp.where(lon > 0, 1.0, 0.0))
    for k in range(LEVELS):
        e, w = all_edges[east_m, k // 2], all_edges[west_m, k // 2]
        if k % 2:
            w = roll(w, -2, 1)
        else:
            e = roll(e, 2, 1)
        ends[k] = jnp.where(easterly, e, w) * exists
    for side in range(2):
        rims[side] = jnp.where(easterly, all_rims[east_m, side], all_rims[west_m, side]) * exists

    for i, b in enumerate((0, tracers)):
        for k in range(LEVELS):
            side_mix[i, k, OWN_ROWS] = roll(ends[k], -(4 * b + 2), 1)
        for side, place in enumerate((RING_ROWS - 1, ROWS)):
            side_mix[i, :, place] = roll(rims[side], -(4 * b + 2), 1)

    levels = range(LEVELS)
    for k in levels:
        stencil = [coef1[i, k] for i in range(5)]
        for i in range(2):
            q = jnp.concatenate([mix[i, k], side_mix[i, k]], axis=1)
            moved[i, k] = advected(q, east(q), west(q), north(q), south(q), stencil)
    tau = jnp.zeros(WIDE, jnp.float32)
    top = tau + 1.0
    for k in levels:
        wet = wets[0, k]
        tau = tau + (0.1 + 0.3 * jnp.maximum(moved[0, k], 0.0))
        below = jnp.exp(-tau)
        light_out[0, k] = (wet * (top - below))[OWN_ROWS, FIRST]
        light = (0.5 * wet) * top
        coef1[5, k] = wet
        coef1[6, k] = light
        moved[0, k] = wet * moved[0, k] + light * moved[1, k]
        top = below
    inner = (OWN_ROWS, FIRST)
    tau = jnp.zeros((ROWS, LANES), jnp.float32)
    top = tau + 1.0
    for k in levels:
        chl = moved[0, k]
        stencil = [coef2[i, k] for i in range(5)]
        after = advected(*(q[inner] for q in (chl, east(chl), west(chl), north(chl), south(chl))), stencil)
        wet = wets[(0, k, *inner)]
        tau = tau + (0.1 + 0.3 * jnp.maximum(after, 0.0))
        below = jnp.exp(-tau)
        coef2[5, k] = wet
        coef2[6, k] = (0.5 * wet) * top
        light_out[1, k] = (2.0 * wet) * (top - below)
        top = below
    for s, heat in enumerate(heats):
        m = lax.rem(lon + (s + 1), n)
        for i in range(2):
            heat[i] = light_out[i, pl.ds(m * share, share)]


def tile_stencil(q, rim, columns, stencil, sub, lane):
    e = jnp.where(lane == LANES - 1, columns, roll(q, -1, 1))
    w = jnp.where(lane == 0, columns, roll(q, 1, 1))
    up = jnp.where(sub == ROWS - 1, rim, roll(q, -1, 0))
    down = jnp.where(sub == 0, rim, roll(q, 1, 0))
    return advected(q, e, w, up, down, stencil)


def swapped(q):
    return jnp.where(iota(q.shape, 1) % 4 == 1, roll(q, -1, 1), roll(q, 1, 1))


def beside_columns(edge, b):
    return roll(edge, LANES - 2 - 4 * b, 1)


def part_of(b, half):
    return slice(b * ROWS, (b + 1) * ROWS), slice(half * LANES, (half + 1) * LANES)


def tile_loop(pairs, source, rims, edge, coef, m_all, adv, store):
    tracers = source.shape[0]
    sub, lane = iota((ROWS, LANES), 0), iota((ROWS, LANES), 1)
    for i in pairs:
        for half in range(2):
            k = 2 * i + half
            stencil = [coef(j, k) for j in range(5)]
            columns = edge[k]
            for b in range(tracers):
                adv[(i, *part_of(b, half))] = tile_stencil(
                    source[b, k], rims[b, k], beside_columns(columns, b), stencil, sub, lane
                )
        react = product(m_all[...], stacked(adv[i], 0))
        for half in range(2):
            k = 2 * i + half
            wet, light = coef(5, k), coef(6, k)
            for b in range(tracers):
                store(b, k, wet * adv[(i, *part_of(b, half))] + light * react[part_of(b, half)])
        yield i


def tracer_kernel(
    n,
    strips,
    f,
    c,
    edges,
    ends,
    rims,
    coef,
    coef2,
    m_all,
    e_all,
    z,
    r,
    u_out,
    v_out,
    result,
    c_out,
    row1,
    edge1,
    row0,
    edge0,
    done,
    adv,
    adv2,
    sem,
    c_sem,
):
    pos = position()
    tracers = c.shape[0]
    lon = pos[1]
    halo = Halo(pos, strips)
    sub, lane = iota((ROWS, LANES), 0), iota((ROWS, LANES), 1)
    easterly = lane % 4 >= 2
    base = LEVELS + n

    rim = row0.at[0]
    rim[:, 0, :] = rims[0]
    rim[:, ROWS - 1, :] = rims[1]
    parts = []
    for k in range(LEVELS):
        q, inside = ends[k], edges[k]
        outer = jnp.where(easterly, roll(q, -1, 1), roll(q, 1, 1))
        inner = jnp.where(easterly, roll(inside, 1, 1), roll(inside, -1, 1))
        up = jnp.where(sub == ROWS - 1, rim[k], roll(q, -1, 0))
        down = jnp.where(sub == 0, rim[k], roll(q, 1, 0))

        def at_edge(i):
            side = coef[i, k, :ROWS, LANES:]
            return (
                jnp.broadcast_to(side[:, :1], (ROWS, LANES)),
                jnp.broadcast_to(side[:, LANES - 1 :], (ROWS, LANES)),
            )

        def pick(pair):
            return jnp.where(easterly, pair[0], pair[1])

        stencil = [pick(at_edge(i)) for i in range(5)]
        wet, light = at_edge(5), at_edge(6)
        moved = advected(
            q, jnp.where(easterly, outer, inner), jnp.where(easterly, inner, outer), up, down, stencil
        )
        parts.append((moved, pick(wet), pick(light)))
        edge0[k] = swapped(q)
    react = product(stacked(jnp.concatenate([p[0] for p in parts], axis=0), 1), e_all[...])
    east_exists = jnp.where(lon < n - 1, 1.0, 0.0)
    west_exists = jnp.where(lon > 0, 1.0, 0.0)
    exists = jnp.where(easterly, east_exists, west_exists)
    for k, (q, wet, light) in enumerate(parts):
        edge1[k] = swapped((wet * q + light * react[k * ROWS : (k + 1) * ROWS]) * exists)

    places = ((0, RING_ROWS - 1), (ROWS - 1, ROWS))
    corners = [swapped(rims[side]) for side in range(2)]
    stencils = [[coef[i, :, place, :LANES] for i in range(7)] for _, place in places]
    for b in range(tracers):
        near = halo.sides(r[base + 2 * b], z[base + 2 * b])
        far = halo.sides(r[base + 2 * b + 1], z[base + 2 * b + 1])
        for side, (at, _) in enumerate(places):
            q = near[side]
            row0[b, :, at, :] = q
            columns = beside_columns(corners[side], b)
            e = jnp.where(lane == LANES - 1, columns, roll(q, -1, 1))
            w = jnp.where(lane == 0, columns, roll(q, 1, 1))
            inner = c[b, :, at, :]
            up, down = (inner, far[side]) if side == 0 else (far[side], inner)
            adv[(LEVELS // 2, *part_of(b, side))] = advected(q, e, w, up, down, stencils[side][:5])
    react = product(m_all[...], stacked(adv[LEVELS // 2], 0))
    for b in range(tracers):
        for side, (at, _) in enumerate(places):
            wet, light = stencils[side][5:]
            row1[b, :, at, :] = wet * adv[(LEVELS // 2, *part_of(b, side))] + light * react[part_of(b, side)]

    def store(b, k, q):
        c_out[b, k] = q

    copies = [pltpu.make_async_copy(f.at[i], ref, sem.at[i]) for i, ref in enumerate((u_out, v_out))]
    for copy in copies:
        copy.start()

    def store_done(b, k, q):
        done[b, k] = q

    pairs = range(LEVELS // 2)
    for _ in tile_loop(pairs, c, row0, edge0, lambda i, k: coef[i, k, :ROWS, :LANES], m_all, adv, store):
        pass
    for i in tile_loop(pairs, c_out, row1, edge1, lambda i, k: coef2[i, k], m_all, adv2, store_done):
        part = pl.ds(2 * i, 2)
        copies.append(pltpu.make_async_copy(done.at[:, part], result.at[:, part], c_sem.at[i]))
        copies[-1].start()
    for copy in copies:
        copy.wait()


def last_kernel(n, *refs):
    others = n - 1
    f, light, heats = refs[0], refs[1], refs[2 : 2 + others]
    t_out, h_out, warm, sem = refs[2 + others :]
    share = f.shape[1]
    _, lon, _ = position()
    here = block_of(lon)
    for level in range(share):
        k = lon * share + level
        warm[0, level, :, here] = f[2, level, :, here] + light[0, k]
        warm[1, level, :, here] = light[1, k]
        for s, heat in enumerate(heats):
            there = block_of(lax.rem(lon + (n - 1 - s), n))
            warm[0, level, :, there] = f[2, level, :, there] + heat[0, level]
            warm[1, level, :, there] = heat[1, level]
    copies = [pltpu.make_async_copy(warm.at[i], ref, sem.at[i]) for i, ref in enumerate((t_out, h_out))]
    for copy in copies:
        copy.start()
    for copy in copies:
        copy.wait()


def shards(groups, n, lats, u, v, t, h, c, count, rates):
    tracers = c.shape[0]
    share, width = u.shape[0], u.shape[2]
    strips = lats * CORES
    vmem = pl.BlockSpec(memory_space=pltpu.VMEM)
    anywhere = pl.BlockSpec(memory_space=pl.ANY)
    hbm = pl.BlockSpec(memory_space=pltpu.HBM)
    params = pltpu.CompilerParams(vmem_limit_bytes=32 * 1024 * 1024)
    dma = pltpu.SemaphoreType.DMA

    def shape(*dims, dtype=jnp.float32):
        return jax.ShapeDtypeStruct(dims, dtype)

    def tiles(*dims):
        return shape(*dims, ROWS, LANES)

    def scratch(*dims):
        return pltpu.VMEM(dims, jnp.float32)

    def call(kernel, name, args, in_specs, out_shape, out_specs=None, scratch_shapes=()):
        return pl.pallas_call(
            kernel,
            out_shape=tuple(out_shape),
            in_specs=in_specs,
            out_specs=out_specs or (vmem,) * len(out_shape),
            scratch_shapes=scratch_shapes,
            compiler_params=params,
            name=name,
        )(*args)

    def permute(q, target):
        pairs = []
        for g in range(groups):
            for a in range(lats):
                for o in range(n):
                    for i in range(CORES):
                        g2, a2, o2, i2 = target(g, a, o, i)
                        pairs.append(
                            (((g * lats + a) * n + o) * CORES + i, ((g2 * lats + a2) * n + o2) * CORES + i2)
                        )
        return lax.ppermute(q, ("grp", "lat", "lon", "role"), pairs)

    def z_target(shift):
        def target(g, a, o, i):
            s = a * CORES + i + (1 if i else -1)
            if 0 <= s < strips:
                return g, s // CORES, (o + shift) % n, s % CORES
            return (g ^ 1 if g ^ 1 < groups else g), a, o, i

        return target

    def x_target(shift):
        return lambda g, a, o, i: (g, a, (o + shift) % n, i)

    def r_target(g, a, o, i):
        return g, a, o, 1 - i

    shifts = range(1, n)
    z_tiles = LEVELS + n + 2 * tracers
    f, c_here, depth, rates, z_pay, r_pay = call(
        functools.partial(load_kernel, n),
        "load",
        [pltpu.with_memory_space_constraint(q, pltpu.HBM) for q in (u, v, t, h, count, rates, c)],
        [hbm] * 7,
        [
            shape(FIELDS, *u.shape),
            shape(*c.shape),
            shape(*count.shape, dtype=jnp.int32),
            shape(*rates.shape),
            tiles(z_tiles),
            tiles(z_tiles),
        ],
        scratch_shapes=[dma((FIELDS + 2,)), dma((4,))],
    )
    r_in = permute(r_pay, r_target)
    z_in = permute(z_pay, z_target(0))
    sums, edges, *pays = call(
        functools.partial(edge_kernel, n),
        "edges",
        (rates, c_here),
        [vmem] * 2,
        [tiles(LEVELS)] * 2 + [tiles(LEVELS // 2)] * (n - 1),
    )
    pays = call(
        functools.partial(join_kernel, n),
        "join",
        (rates, f, z_pay, r_in, *pays),
        [vmem] * (n + 3),
        [tiles(FIELDS * share + LEVELS // 2 + share + 2)] * (n - 1) + [tiles(share + 1)] * (n - 1),
    )
    xs = [permute(q, x_target(s)) for s, q in zip(shifts, pays[: n - 1])]
    xzs = [permute(q, z_target(s)) for s, q in zip(shifts, pays[n - 1 :])]

    m_size, e_size = tracers * ROWS, LANES
    bf16 = jnp.bfloat16
    m_all, e_all = call(
        spread_kernel,
        "spread",
        (rates,),
        [vmem],
        [shape(m_size, 3 * m_size, dtype=bf16), shape(3 * e_size, e_size, dtype=bf16)],
    )

    args = (rates, f, depth, c_here, sums, z_in, r_in)
    own1, own2, wets, mix, f_new = call(
        functools.partial(own_kernel, n, strips),
        "own",
        args,
        [vmem] * len(args),
        [
            shape(5, share, RING_ROWS, RING_COLS),
            tiles(5, share),
            shape(3, LEVELS, RING_ROWS, RING_COLS),
            shape(2, LEVELS, RING_ROWS, LANES),
            shape(3, *u.shape),
        ],
        scratch_shapes=[scratch(FIELDS, share, RING_ROWS, RING_COLS), scratch(RING_ROWS, RING_COLS)],
    )
    args = (own1, own2, wets, mix, m_all, e_all, *xs, *xzs)
    coef1, coef2, ends, rims, light, *heats = call(
        functools.partial(flow_kernel, n, strips, tracers),
        "flow",
        args,
        [vmem] * len(args),
        [
            shape(7, LEVELS, RING_ROWS, RING_COLS),
            tiles(7, LEVELS),
            tiles(LEVELS),
            shape(2, LEVELS, LANES),
            tiles(2, LEVELS),
        ]
        + [tiles(2, share)] * (n - 1),
        scratch_shapes=[
            scratch(FIELDS, (n - 1) * share, RING_ROWS, RING_COLS),
            scratch(2, LEVELS, RING_ROWS, LANES),
            scratch(n, LEVELS // 2, ROWS, LANES),
            scratch(n, 2, LEVELS, LANES),
            scratch(2, LEVELS, RING_ROWS, RING_COLS),
        ],
    )
    heats = [permute(q, x_target(s)) for s, q in zip(shifts, heats)]
    args = (f_new, c_here, edges, ends, rims, coef1, coef2, m_all, e_all, z_in, r_in)
    u_new, v_new, c_new = call(
        functools.partial(tracer_kernel, n, strips),
        "tracers",
        args,
        [vmem] * len(args),
        [shape(*u.shape)] * 2 + [shape(*c.shape)],
        out_specs=(anywhere,) * 3,
        scratch_shapes=[
            scratch(*c.shape),
            scratch(tracers, LEVELS, ROWS, LANES),
            scratch(LEVELS, ROWS, LANES),
            scratch(tracers, LEVELS, ROWS, LANES),
            scratch(LEVELS, ROWS, LANES),
            scratch(*c.shape),
            scratch(LEVELS // 2 + 1, tracers * ROWS, 2 * LANES),
            scratch(LEVELS // 2, tracers * ROWS, 2 * LANES),
            dma((2,)),
            dma((LEVELS // 2,)),
        ],
    )
    args = (f_new, light, *heats)
    t_new, h_new = call(
        functools.partial(last_kernel, n),
        "last",
        args,
        [vmem] * len(args),
        [shape(*u.shape)] * 2,
        out_specs=(anywhere,) * 2,
        scratch_shapes=[scratch(2, *u.shape), dma((2,))],
    )
    return u_new, v_new, t_new, h_new, c_new


def solution(mesh):
    level = P("lon", ("grp", "lat", "role"), None)
    tracer = P(None, None, ("grp", "lat", "role"), "lon")
    return jax.shard_map(
        functools.partial(shards, mesh.shape["grp"], mesh.shape["lon"], mesh.shape["lat"]),
        mesh=mesh,
        in_specs=(level, level, level, level, tracer, P(("grp", "lat", "role"), None), P()),
        out_specs=(level, level, level, level, tracer),
        check_vma=False,
    )
```

```python
import functools

import jax
import jax.numpy as jnp
from jax import lax
from jax.experimental import pallas as pl
from jax.experimental.pallas import tpu as pltpu
from jax.sharding import PartitionSpec as P

ROWS = 8
LANES = 128
LEVELS = 8
CORES = 2
FIELDS = 4
NEAR = 3

RING_ROWS = 2 * ROWS
RING_COLS = 2 * LANES


def iota(shape, dim):
    return lax.broadcasted_iota(jnp.int32, shape, dim)


def roll(q, shift, axis):
    return pltpu.roll(q, shift % q.shape[axis], axis)


def position():
    lat, lon, role = lax.axis_index("lat"), lax.axis_index("lon"), lax.axis_index("role")
    return lat * CORES + role, lon, role


def block_of(m):
    return pl.ds(pl.multiple_of(m * LANES, LANES), LANES)


def packed(tracers, rates, tiles):
    lane = iota((ROWS, LANES), 1)
    zero = jnp.zeros((ROWS, LANES), jnp.float32)
    total, edge = [zero] * len(tiles), [zero] * len(tiles)
    for b in range(tracers):
        rate = jnp.broadcast_to(rates[:1, b : b + 1], (ROWS, LANES))
        mine = lane // 4 == b
        for i, get in enumerate(tiles):
            q = get(b)
            total[i] = total[i] + rate * q
            edge[i] = jnp.where(mine, roll(q, 4 * b + 2, 1), edge[i])
    mine = lane // 4 == tracers
    return total, [jnp.where(mine, roll(t, 4 * tracers + 2, 1), e) for t, e in zip(total, edge)]


def last_rows(tiles):
    u, v, t, h = tiles
    sub = iota((ROWS, LANES), 0)
    low = jnp.where(sub >= 1, roll(t, -5, 0), roll(h, 1, 0))
    return jnp.where(sub >= 5, v, jnp.where(sub >= 3, roll(u, -3, 0), low))


def first_rows(tiles):
    u, v, t, h = tiles
    sub = iota((ROWS, LANES), 0)
    high = jnp.where(sub <= 6, roll(t, 5, 0), roll(h, -1, 0))
    return jnp.where(sub <= 2, v, jnp.where(sub <= 4, roll(u, 3, 0), high))


def next_rows(south, north, field):
    shift = (3, 0, 5, -1)[field]
    if shift:
        south, north = roll(south, shift, 0), roll(north, -shift, 0)
    return jnp.where(iota((ROWS, LANES), 0) >= ROWS // 2, south, north)


def sides_of(get, amount, east, west, into, start):
    lane = iota((ROWS, LANES), 1)
    for i in range(amount):
        first = start + 2 * NEAR * i
        side = jnp.where(lane < LANES // 2, get(i, east), get(i, west))
        into = jnp.where((lane >= first) & (lane < first + 2 * NEAR), roll(side, first + NEAR, 1), into)
    return into


def side_in(tile, i, start):
    return roll(tile, -(start + 2 * NEAR * i + NEAR), 1)


def load_kernel(n, u, v, t, h, count, rates, c, f_out, c_out, d_out, rates_out, z_out, r_out, f_sem, c_sem):
    tracers, share = c.shape[0], f_out.shape[1]
    _, _, role = position()
    upper = role == 1
    copies = [pltpu.make_async_copy(ref, f_out.at[i], f_sem.at[i]) for i, ref in enumerate((u, v, t, h))]
    copies.append(pltpu.make_async_copy(count, d_out, f_sem.at[FIELDS]))
    copies.append(pltpu.make_async_copy(rates, rates_out, f_sem.at[FIELDS + 1]))
    batch = tracers // c_sem.shape[0]
    c_copies = []
    for i in range(c_sem.shape[0]):
        part = pl.ds(i * batch, batch)
        c_copies.append(pltpu.make_async_copy(c.at[part], c_out.at[part], c_sem.at[i]))
    for copy in copies + c_copies:
        copy.start()
    for copy in copies:
        copy.wait()

    def whole(i, block):
        return f_out[i // share, i % share, :, block_of(block)]

    def strips_of(level, block):
        tiles = [whole(field * share + level, block) for field in range(FIELDS)]
        top, bottom = last_rows(tiles), first_rows(tiles)
        return jnp.where(upper, top, bottom), jnp.where(upper, bottom, top)

    count_f = FIELDS * share
    for level in range(share):
        for block in range(n):
            z_out[level * n + block], r_out[level * n + block] = strips_of(level, block)
    base = LEVELS
    for block in range(n):
        depth = d_out[:, block * LANES : (block + 1) * LANES].astype(jnp.float32)
        z_out[base + block] = depth
        r_out[base + block] = depth
    base += n
    for i, copy in enumerate(c_copies):
        copy.wait()
        for b in range(i * batch, (i + 1) * batch):
            for far in range(2):
                bottom, top = c_out[b, :, far, :], c_out[b, :, ROWS - 1 - far, :]
                z_out[base + 2 * b + far] = jnp.where(upper, top, bottom)
                r_out[base + 2 * b + far] = jnp.where(upper, bottom, top)


def edge_kernel(n, rates, c, sums, edges, *outs):
    _, lon, _ = position()
    total, edge = packed(c.shape[0], rates, [lambda b, k=k: c[b, k] for k in range(LEVELS)])
    for k in range(LEVELS):
        sums[k], edges[k] = total[k], edge[k]
    low = iota((ROWS, LANES), 1) % 4 < 2
    for s, out in enumerate(outs):
        to_east = lax.rem(lon + (s + 1), n) > lon
        for i in range(LEVELS // 2):
            a, b = (jnp.where(to_east, q, roll(q, -2, 1)) for q in (edge[2 * i], edge[2 * i + 1]))
            out[i] = jnp.where(low, a, roll(b, 2, 1))


def join_kernel(n, rates, f, z, r, *refs):
    pays, x_outs, xz_outs = (refs[i * (n - 1) : (i + 1) * (n - 1)] for i in range(3))
    _, lon, _ = position()
    tracers, share, base = rates.shape[0], LEVELS // n, LEVELS + n
    _, (rim_r, rim_z) = packed(tracers, rates, [lambda b: r[base + 2 * b], lambda b: z[base + 2 * b]])
    zero = jnp.zeros((ROWS, LANES), jnp.float32)
    count = FIELDS * share

    def whole(i, block):
        return f[i // share, i % share, :, block_of(block)]

    for s, (pay, x, xz) in enumerate(zip(pays, x_outs, xz_outs)):
        m = lax.rem(lon + (s + 1), n)
        e, w = lax.rem(m + 1, n), lax.rem(m + n - 1, n)
        for i in range(count):
            x[i] = whole(i, m)
        x[count : count + LEVELS // 2] = pay[...]
        end = count + LEVELS // 2
        for level in range(share):
            x[end + level] = r[level * n + m]
            xz[level] = z[level * n + m]
        x[end + share] = rim_r
        sides = sides_of(whole, count, e, w, zero, 0)
        x[end + share + 1] = sides_of(
            lambda level, block: r[level * n + block], share, e, w, sides, 2 * NEAR * count
        )
        xz[share] = sides_of(lambda level, block: z[level * n + block], share, e, w, rim_z, 4 * (tracers + 1))


def split(q):
    high = q.astype(jnp.bfloat16)
    return high, (q - high.astype(jnp.float32)).astype(jnp.bfloat16)


def spread_kernel(rates, m_all, e_all):
    tracers = rates.shape[0]
    for group, transposed, size, out in ((ROWS, False, m_all.shape[0], m_all), (4, True, e_all.shape[1], e_all)):
        rows = (iota((size, tracers), 0) // group == iota((size, tracers), 1)).astype(jnp.bfloat16)
        cols = (iota((tracers, size), 1) // group == iota((tracers, size), 0)).astype(jnp.bfloat16)
        same = iota((size, size), 0) % group == iota((size, size), 1) % group
        parts = []
        for q in split(rates[...].T if transposed else rates[...]):
            wide = product(product(rows, q).astype(jnp.bfloat16), cols)
            parts.append(jnp.where(same, wide, 0.0).astype(jnp.bfloat16))
        high, low = parts
        out[...] = jnp.concatenate([high, high, low], axis=0 if transposed else 1)


def stacked(q, axis):
    high, low = split(q)
    return jnp.concatenate([high, low, high], axis=axis)


def product(left, right):
    return jnp.dot(left, right, preferred_element_type=jnp.float32)


def advected(q, e, w, up, down, stencil):
    a0, mu, pw, mv, ps = stencil
    return (a0 * q + (pw * w - mu * e)) + (ps * down - mv * up)


class Halo:
    def __init__(self, pos, strips):
        self.upper = pos[2] == 1
        end = jnp.logical_or(
            jnp.logical_and(pos[0] == 0, jnp.logical_not(self.upper)),
            jnp.logical_and(pos[0] == strips - 1, self.upper),
        )
        self.keep_z = jnp.where(end, 0.0, 1.0)
        self.from_r = (iota((ROWS, LANES), 0) >= ROWS // 2) == self.upper

    def rows(self, r, z):
        return jnp.where(self.from_r, r, z * self.keep_z)

    def sides(self, r, z):
        z = z * self.keep_z
        return jnp.where(self.upper, r, z), jnp.where(self.upper, z, r)


FIRST, SECOND = slice(0, LANES), slice(LANES, RING_COLS)
OWN_ROWS, FAR_ROWS = slice(0, ROWS), slice(ROWS, RING_ROWS)
WIDE = (RING_ROWS, RING_COLS)


def put(ref, at, tiles):
    places = ((OWN_ROWS, FIRST), (OWN_ROWS, SECOND), (FAR_ROWS, FIRST), (FAR_ROWS, SECOND))
    for tile, (rows, cols) in zip(tiles, places):
        ref[(*at, rows, cols)] = tile


def beside(m, n):
    return lax.rem(m + 1, n), lax.rem(m + n - 1, n)


def north(q):
    return roll(q, -1, 0)


def south(q):
    return roll(q, 1, 0)


def east(q):
    return roll(q, -1, 1)


def west(q):
    return roll(q, 1, 1)


def around(m, n):
    e, w = beside(m, n)
    ring_col = iota(WIDE, 1)
    block = jnp.where(ring_col < LANES, m, jnp.where(ring_col < LANES + LANES // 2, e, w))
    col = block * LANES + ring_col % LANES
    not_last, not_first = col < n * LANES - 1, col > 0
    return lambda q: jnp.where(not_last, east(q), 0.0), lambda q: jnp.where(not_first, west(q), 0.0)


def coriolis(strip, strips):
    ring_row = iota(WIDE, 0)
    row = strip * ROWS + jnp.where(ring_row < ROWS + ROWS // 2, ring_row, ring_row - RING_ROWS)
    return 0.3 * (2.0 * (row.astype(jnp.float32) + 0.5) / (strips * ROWS) - 1.0)


def masks(k, counts, east_of):
    wet = jnp.where(counts > k, 1.0, 0.0)
    return wet, wet * east_of(wet), wet * north(wet)


def advance(uu, vv, tt, wet_u, wet_v, turn, east_of, west_of, again):
    def mixed(q, e, w, nn):
        return 0.6 * q + 0.1 * ((e + w) + (nn + south(q)))

    te, tn = east_of(tt), north(tt)
    u_west = west(uu) if again else west_of(uu)
    u_new = wet_u * (mixed(uu, east(uu), u_west, north(uu)) + (turn * vv - 0.2 * (te - tt)))
    v_new = wet_v * (mixed(vv, east_of(vv), west_of(vv), north(vv)) - (turn * uu + 0.2 * (tn - tt)))
    return u_new, v_new, mixed(tt, te, west_of(tt), tn)


def coefficients(uu, vv):
    uu, vv = 0.5 * uu, 0.5 * vv
    uw, vs = west(uu), south(vv)
    pw, ps = jnp.maximum(uw, 0.0), jnp.maximum(vs, 0.0)
    mu, mv = jnp.minimum(uu, 0.0), jnp.minimum(vv, 0.0)
    a0 = (1.0 - (jnp.maximum(uu, 0.0) - jnp.minimum(uw, 0.0))) - (jnp.maximum(vv, 0.0) - jnp.minimum(vs, 0.0))
    return a0, mu, pw, mv, ps


def two_steps(read, wets, turn, shifts):
    uu, vv, tt = advance(read(0), read(1), read(2), *wets[1:], turn, *shifts, False)
    tt = wets[0] * (tt + 0.5 * read(3))
    stencil = coefficients(uu, vv)
    uu, vv, tt = advance(uu, vv, tt, *wets[1:], turn, *shifts, True)
    return uu, vv, wets[0] * tt, stencil, [q[OWN_ROWS, FIRST] for q in coefficients(uu, vv)]


def own_kernel(n, strips, rates, f, count, c, sums, z, r, coef1, coef2, wets, mix, f_out, dyn, depth):
    tracers, share = c.shape[0], f.shape[1]
    strip, lon, _ = pos = position()
    halo = Halo(pos, strips)
    lane = iota((ROWS, LANES), 1)
    base = LEVELS + n

    def window(main, near, m):
        e, w = beside(m, n)

        def side(g):
            return g(e) if n == 2 else jnp.where(lane < LANES // 2, g(e), g(w))

        return main(m), side(main), near(m), side(near)

    def own_window(field, level, m):
        def near(block):
            return next_rows(*halo.sides(r[level * n + block], z[level * n + block]), field)

        return window(lambda block: f[field, level, :, block_of(block)], near, m)

    def depth_window(m):
        return window(
            lambda block: count[:, block_of(block)].astype(jnp.float32),
            lambda block: halo.rows(r[LEVELS + block], z[LEVELS + block]),
            m,
        )

    put(depth, (), depth_window(lon))
    for field in range(FIELDS):
        for level in range(share):
            put(dyn, (field, level), own_window(field, level, lon))
    turn = coriolis(strip, strips)
    shifts = around(lon, n)
    for k in range(LEVELS):
        for i, q in enumerate(masks(float(k), depth[...], shifts[0])):
            wets[i, k] = q

    def one_level(level, carry):
        wet = [wets[i, lon * share + level] for i in range(3)]
        uu, vv, tt, stencil, stencil2 = two_steps(lambda i: dyn[i, level], wet, turn, shifts)
        for i, q in enumerate(stencil):
            coef1[i, level] = q
        for i, q in enumerate(stencil2):
            coef2[i, level] = q
        for i, q in enumerate((uu, vv, tt)):
            f_out[i, level, :, block_of(lon)] = q[OWN_ROWS, FIRST]
            if n == 2:
                f_out[i, level, :, block_of(1 - lon)] = q[OWN_ROWS, SECOND]
        return carry

    lax.fori_loop(0, share, one_level, 0, unroll=min(2, share))

    mix[0, :, OWN_ROWS] = c[0]
    mix[1, :, OWN_ROWS] = sums[...]
    for far in range(2):
        total = [jnp.zeros((LEVELS, LANES), jnp.float32)] * 2
        for b in range(tracers):
            rows = halo.sides(r[base + 2 * b + far], z[base + 2 * b + far])
            if b == 0:
                chl = rows
            rate = jnp.broadcast_to(rates[:1, b : b + 1], (ROWS, LANES))
            total = [a + rate * q for a, q in zip(total, rows)]
        for i, rows in enumerate((chl, total)):
            mix[i, :, RING_ROWS - 1 - far] = rows[0]
            mix[i, :, ROWS + far] = rows[1]

    if n > 2:

        def other_block(s, carry):
            m = lax.rem(lon + s, n)
            around_m = around(m, n)
            put(depth, (), depth_window(m))
            for level in range(share):
                k = (lon * share + level).astype(jnp.float32)
                for field in range(FIELDS):
                    put(dyn, (field, level), own_window(field, level, m))
                wet = masks(k, depth[...], around_m[0])
                after = two_steps(lambda i, level=level: dyn[i, level], wet, turn, around_m)
                for i, q in enumerate(after[:3]):
                    f_out[i, level, :, block_of(m)] = q[OWN_ROWS, FIRST]
            return carry

        lax.fori_loop(1, n, other_block, 0)


def flow_kernel(n, strips, tracers, *refs):
    own1, own2, wets, mix = refs[:4]
    others = n - 1
    xs, xzs = (refs[6 + i * others : 6 + (i + 1) * others] for i in range(2))
    coef1, coef2, ends, rims, light_out = refs[6 + 2 * others : 11 + 2 * others]
    heats = refs[11 + 2 * others : 11 + 3 * others]
    dyn, side_mix, all_edges, all_rims, moved = refs[11 + 3 * others :]
    share = own1.shape[1]
    strip, lon, _ = pos = position()
    halo = Halo(pos, strips)
    lane = iota((ROWS, LANES), 1)
    turn = coriolis(strip, strips)
    shifts = around(lon, n)
    mine = pl.ds(lon * share, share)
    for i in range(5):
        coef1[i, mine] = own1[i]
        coef2[i, mine] = own2[i]

    fields = FIELDS * share
    end = fields + LEVELS // 2
    last_lane = 4 * (tracers + 1)
    for s, (x, xz) in enumerate(zip(xs, xzs)):
        m = lax.rem(lon + (n - 1 - s), n)
        sides, far_sides = x[end + share + 1], xz[share]
        for level in range(share):
            near = halo.sides(x[end + level], xz[level])
            corners = halo.sides(side_in(sides, level, 2 * NEAR * fields), side_in(far_sides, level, last_lane))
            for field in range(FIELDS):
                i = field * share + level
                put(
                    dyn,
                    (field, s * share + level),
                    (x[i], side_in(sides, i, 0), next_rows(*near, field), next_rows(*corners, field)),
                )
        all_edges[m] = x[fields:end]
        all_rims[m, 0], all_rims[m, 1] = halo.sides(x[end + share], far_sides)

    def other_level(i):
        s, level = i // share, i % share
        k = lax.rem(lon + (n - 1 - s), n) * share + level
        wet = [wets[j, k] for j in range(3)]
        _, _, _, stencil, stencil2 = two_steps(lambda j: dyn[j, i], wet, turn, shifts)
        for j, q in enumerate(stencil):
            coef1[j, k] = q
        for j, q in enumerate(stencil2):
            coef2[j, k] = q

    for i in range(others * share):
        other_level(i)

    east_m, west_m = beside(lon, n)
    easterly = lane % 4 >= 2
    exists = jnp.where(easterly, jnp.where(lon < n - 1, 1.0, 0.0), jnp.where(lon > 0, 1.0, 0.0))
    for k in range(LEVELS):
        e, w = all_edges[east_m, k // 2], all_edges[west_m, k // 2]
        if k % 2:
            w = roll(w, -2, 1)
        else:
            e = roll(e, 2, 1)
        ends[k] = jnp.where(easterly, e, w) * exists
    for side in range(2):
        rims[side] = jnp.where(easterly, all_rims[east_m, side], all_rims[west_m, side]) * exists

    for i, b in enumerate((0, tracers)):
        for k in range(LEVELS):
            side_mix[i, k, OWN_ROWS] = roll(ends[k], -(4 * b + 2), 1)
        for side, place in enumerate((RING_ROWS - 1, ROWS)):
            side_mix[i, :, place] = roll(rims[side], -(4 * b + 2), 1)

    levels = range(LEVELS)
    for k in levels:
        stencil = [coef1[i, k] for i in range(5)]
        for i in range(2):
            q = jnp.concatenate([mix[i, k], side_mix[i, k]], axis=1)
            moved[i, k] = advected(q, east(q), west(q), north(q), south(q), stencil)
    tau = jnp.zeros(WIDE, jnp.float32)
    top = tau + 1.0
    for k in levels:
        wet = wets[0, k]
        tau = tau + (0.1 + 0.3 * jnp.maximum(moved[0, k], 0.0))
        below = jnp.exp(-tau)
        light_out[0, k] = (wet * (top - below))[OWN_ROWS, FIRST]
        light = (0.5 * wet) * top
        coef1[5, k] = wet
        coef1[6, k] = light
        moved[0, k] = wet * moved[0, k] + light * moved[1, k]
        top = below
    inner = (OWN_ROWS, FIRST)
    tau = jnp.zeros((ROWS, LANES), jnp.float32)
    top = tau + 1.0
    for k in levels:
        chl = moved[0, k]
        stencil = [coef2[i, k] for i in range(5)]
        after = advected(*(q[inner] for q in (chl, east(chl), west(chl), north(chl), south(chl))), stencil)
        wet = wets[(0, k, *inner)]
        tau = tau + (0.1 + 0.3 * jnp.maximum(after, 0.0))
        below = jnp.exp(-tau)
        coef2[5, k] = wet
        coef2[6, k] = (0.5 * wet) * top
        light_out[1, k] = (2.0 * wet) * (top - below)
        top = below
    for s, heat in enumerate(heats):
        m = lax.rem(lon + (s + 1), n)
        for i in range(2):
            heat[i] = light_out[i, pl.ds(m * share, share)]


def tile_stencil(q, rim, columns, stencil, sub, lane):
    e = jnp.where(lane == LANES - 1, columns, roll(q, -1, 1))
    w = jnp.where(lane == 0, columns, roll(q, 1, 1))
    up = jnp.where(sub == ROWS - 1, rim, roll(q, -1, 0))
    down = jnp.where(sub == 0, rim, roll(q, 1, 0))
    return advected(q, e, w, up, down, stencil)


def swapped(q):
    return jnp.where(iota(q.shape, 1) % 4 == 1, roll(q, -1, 1), roll(q, 1, 1))


def beside_columns(edge, b):
    return roll(edge, LANES - 2 - 4 * b, 1)


def part_of(b, half):
    return slice(b * ROWS, (b + 1) * ROWS), slice(half * LANES, (half + 1) * LANES)


def tile_loop(pairs, source, rims, edge, coef, m_all, adv, store):
    tracers = source.shape[0]
    sub, lane = iota((ROWS, LANES), 0), iota((ROWS, LANES), 1)
    for i in pairs:
        for half in range(2):
            k = 2 * i + half
            stencil = [coef(j, k) for j in range(5)]
            columns = edge[k]
            for b in range(tracers):
                adv[(i, *part_of(b, half))] = tile_stencil(
                    source[b, k], rims[b, k], beside_columns(columns, b), stencil, sub, lane
                )
        react = product(m_all[...], stacked(adv[i], 0))
        for half in range(2):
            k = 2 * i + half
            wet, light = coef(5, k), coef(6, k)
            for b in range(tracers):
                store(b, k, wet * adv[(i, *part_of(b, half))] + light * react[part_of(b, half)])
        yield i


def tracer_kernel(
    n,
    strips,
    c,
    edges,
    ends,
    rims,
    coef,
    coef2,
    m_all,
    e_all,
    z,
    r,
    done,
    c_out,
    row1,
    edge1,
    row0,
    edge0,
    rim,
    adv,
    adv2,
):
    pos = position()
    tracers = c.shape[0]
    lon = pos[1]
    halo = Halo(pos, strips)
    sub, lane = iota((ROWS, LANES), 0), iota((ROWS, LANES), 1)
    easterly = lane % 4 >= 2
    base = LEVELS + n

    rim[:, 0, :] = rims[0]
    rim[:, ROWS - 1, :] = rims[1]
    parts = []
    for k in range(LEVELS):
        q, inside = ends[k], edges[k]
        outer = jnp.where(easterly, roll(q, -1, 1), roll(q, 1, 1))
        inner = jnp.where(easterly, roll(inside, 1, 1), roll(inside, -1, 1))
        up = jnp.where(sub == ROWS - 1, rim[k], roll(q, -1, 0))
        down = jnp.where(sub == 0, rim[k], roll(q, 1, 0))

        def at_edge(i):
            side = coef[i, k, :ROWS, LANES:]
            return (
                jnp.broadcast_to(side[:, :1], (ROWS, LANES)),
                jnp.broadcast_to(side[:, LANES - 1 :], (ROWS, LANES)),
            )

        def pick(pair):
            return jnp.where(easterly, pair[0], pair[1])

        stencil = [pick(at_edge(i)) for i in range(5)]
        wet, light = at_edge(5), at_edge(6)
        moved = advected(
            q, jnp.where(easterly, outer, inner), jnp.where(easterly, inner, outer), up, down, stencil
        )
        parts.append((moved, pick(wet), pick(light)))
        edge0[k] = swapped(q)
    react = product(stacked(jnp.concatenate([p[0] for p in parts], axis=0), 1), e_all[...])
    east_exists = jnp.where(lon < n - 1, 1.0, 0.0)
    west_exists = jnp.where(lon > 0, 1.0, 0.0)
    exists = jnp.where(easterly, east_exists, west_exists)
    for k, (q, wet, light) in enumerate(parts):
        edge1[k] = swapped((wet * q + light * react[k * ROWS : (k + 1) * ROWS]) * exists)

    places = ((0, RING_ROWS - 1), (ROWS - 1, ROWS))
    corners = [swapped(rims[side]) for side in range(2)]
    stencils = [[coef[i, :, place, :LANES] for i in range(7)] for _, place in places]
    for b in range(tracers):
        near = halo.sides(r[base + 2 * b], z[base + 2 * b])
        far = halo.sides(r[base + 2 * b + 1], z[base + 2 * b + 1])
        for side, (at, _) in enumerate(places):
            q = near[side]
            row0[b, :, at, :] = q
            columns = beside_columns(corners[side], b)
            e = jnp.where(lane == LANES - 1, columns, roll(q, -1, 1))
            w = jnp.where(lane == 0, columns, roll(q, 1, 1))
            inner = c[b, :, at, :]
            up, down = (inner, far[side]) if side == 0 else (far[side], inner)
            adv[(LEVELS // 2, *part_of(b, side))] = advected(q, e, w, up, down, stencils[side][:5])
    react = product(m_all[...], stacked(adv[LEVELS // 2], 0))
    for b in range(tracers):
        for side, (at, _) in enumerate(places):
            wet, light = stencils[side][5:]
            row1[b, :, at, :] = wet * adv[(LEVELS // 2, *part_of(b, side))] + light * react[part_of(b, side)]

    def store(b, k, q):
        c_out[b, k] = q

    def store_done(b, k, q):
        done[b, k] = q

    pairs = range(LEVELS // 2)
    for _ in tile_loop(pairs, c, row0, edge0, lambda i, k: coef[i, k, :ROWS, :LANES], m_all, adv, store):
        pass
    for _ in tile_loop(pairs, c_out, row1, edge1, lambda i, k: coef2[i, k], m_all, adv2, store_done):
        pass


def last_kernel(n, *refs):
    others = n - 1
    c, f, light, heats = *refs[:3], refs[3 : 3 + others]
    c_out, u_out, v_out, t_out, h_out, warm, sem, c_sem = refs[3 + others :]
    copies = [pltpu.make_async_copy(f.at[i], ref, sem.at[i]) for i, ref in enumerate((u_out, v_out))]
    batch = c.shape[0] // c_sem.shape[0]
    for i in range(c_sem.shape[0]):
        part = pl.ds(i * batch, batch)
        copies.append(pltpu.make_async_copy(c.at[part], c_out.at[part], c_sem.at[i]))
    for copy in copies:
        copy.start()
    share = f.shape[1]
    _, lon, _ = position()
    here = block_of(lon)
    for level in range(share):
        k = lon * share + level
        warm[0, level, :, here] = f[2, level, :, here] + light[0, k]
        warm[1, level, :, here] = light[1, k]
        for s, heat in enumerate(heats):
            there = block_of(lax.rem(lon + (n - 1 - s), n))
            warm[0, level, :, there] = f[2, level, :, there] + heat[0, level]
            warm[1, level, :, there] = heat[1, level]
    copies += [pltpu.make_async_copy(warm.at[i], ref, sem.at[2 + i]) for i, ref in enumerate((t_out, h_out))]
    for copy in copies[-2:]:
        copy.start()
    for copy in copies:
        copy.wait()


def shards(groups, n, lats, u, v, t, h, c, count, rates):
    tracers = c.shape[0]
    share, width = u.shape[0], u.shape[2]
    strips = lats * CORES
    vmem = pl.BlockSpec(memory_space=pltpu.VMEM)
    anywhere = pl.BlockSpec(memory_space=pl.ANY)
    hbm = pl.BlockSpec(memory_space=pltpu.HBM)
    params = pltpu.CompilerParams(vmem_limit_bytes=32 * 1024 * 1024)
    dma = pltpu.SemaphoreType.DMA

    def shape(*dims, dtype=jnp.float32):
        return jax.ShapeDtypeStruct(dims, dtype)

    def tiles(*dims):
        return shape(*dims, ROWS, LANES)

    def scratch(*dims):
        return pltpu.VMEM(dims, jnp.float32)

    def call(kernel, name, args, in_specs, out_shape, out_specs=None, scratch_shapes=()):
        return pl.pallas_call(
            kernel,
            out_shape=tuple(out_shape),
            in_specs=in_specs,
            out_specs=out_specs or (vmem,) * len(out_shape),
            scratch_shapes=scratch_shapes,
            compiler_params=params,
            name=name,
        )(*args)

    def permute(q, target):
        pairs = []
        for g in range(groups):
            for a in range(lats):
                for o in range(n):
                    for i in range(CORES):
                        g2, a2, o2, i2 = target(g, a, o, i)
                        pairs.append(
                            (((g * lats + a) * n + o) * CORES + i, ((g2 * lats + a2) * n + o2) * CORES + i2)
                        )
        return lax.ppermute(q, ("grp", "lat", "lon", "role"), pairs)

    def z_target(shift):
        def target(g, a, o, i):
            s = a * CORES + i + (1 if i else -1)
            if 0 <= s < strips:
                return g, s // CORES, (o + shift) % n, s % CORES
            return (g ^ 1 if g ^ 1 < groups else g), a, o, i

        return target

    def x_target(shift):
        return lambda g, a, o, i: (g, a, (o + shift) % n, i)

    def r_target(g, a, o, i):
        return g, a, o, 1 - i

    shifts = range(1, n)
    z_tiles = LEVELS + n + 2 * tracers
    f, c_here, depth, rates, z_pay, r_pay = call(
        functools.partial(load_kernel, n),
        "load",
        [pltpu.with_memory_space_constraint(q, pltpu.HBM) for q in (u, v, t, h, count, rates, c)],
        [hbm] * 7,
        [
            shape(FIELDS, *u.shape),
            shape(*c.shape),
            shape(*count.shape, dtype=jnp.int32),
            shape(*rates.shape),
            tiles(z_tiles),
            tiles(z_tiles),
        ],
        scratch_shapes=[dma((FIELDS + 2,)), dma((4,))],
    )
    r_in = permute(r_pay, r_target)
    z_in = permute(z_pay, z_target(0))
    sums, edges, *pays = call(
        functools.partial(edge_kernel, n),
        "edges",
        (rates, c_here),
        [vmem] * 2,
        [tiles(LEVELS)] * 2 + [tiles(LEVELS // 2)] * (n - 1),
    )
    pays = call(
        functools.partial(join_kernel, n),
        "join",
        (rates, f, z_pay, r_in, *pays),
        [vmem] * (n + 3),
        [tiles(FIELDS * share + LEVELS // 2 + share + 2)] * (n - 1) + [tiles(share + 1)] * (n - 1),
    )
    xs = [permute(q, x_target(s)) for s, q in zip(shifts, pays[: n - 1])]
    xzs = [permute(q, z_target(s)) for s, q in zip(shifts, pays[n - 1 :])]

    m_size, e_size = tracers * ROWS, LANES
    bf16 = jnp.bfloat16
    m_all, e_all = call(
        spread_kernel,
        "spread",
        (rates,),
        [vmem],
        [shape(m_size, 3 * m_size, dtype=bf16), shape(3 * e_size, e_size, dtype=bf16)],
    )

    args = (rates, f, depth, c_here, sums, z_in, r_in)
    own1, own2, wets, mix, f_new = call(
        functools.partial(own_kernel, n, strips),
        "own",
        args,
        [vmem] * len(args),
        [
            shape(5, share, RING_ROWS, RING_COLS),
            tiles(5, share),
            shape(3, LEVELS, RING_ROWS, RING_COLS),
            shape(2, LEVELS, RING_ROWS, LANES),
            shape(3, *u.shape),
        ],
        scratch_shapes=[scratch(FIELDS, share, RING_ROWS, RING_COLS), scratch(RING_ROWS, RING_COLS)],
    )
    args = (own1, own2, wets, mix, m_all, e_all, *xs, *xzs)
    coef1, coef2, ends, rims, light, *heats = call(
        functools.partial(flow_kernel, n, strips, tracers),
        "flow",
        args,
        [vmem] * len(args),
        [
            shape(7, LEVELS, RING_ROWS, RING_COLS),
            tiles(7, LEVELS),
            tiles(LEVELS),
            shape(2, LEVELS, LANES),
            tiles(2, LEVELS),
        ]
        + [tiles(2, share)] * (n - 1),
        scratch_shapes=[
            scratch(FIELDS, (n - 1) * share, RING_ROWS, RING_COLS),
            scratch(2, LEVELS, RING_ROWS, LANES),
            scratch(n, LEVELS // 2, ROWS, LANES),
            scratch(n, 2, LEVELS, LANES),
            scratch(2, LEVELS, RING_ROWS, RING_COLS),
        ],
    )
    heats = [permute(q, x_target(s)) for s, q in zip(shifts, heats)]
    args = (c_here, edges, ends, rims, coef1, coef2, m_all, e_all, z_in, r_in)
    (c_new,) = call(
        functools.partial(tracer_kernel, n, strips),
        "tracers",
        args,
        [vmem] * len(args),
        [shape(*c.shape)],
        scratch_shapes=[
            scratch(*c.shape),
            scratch(tracers, LEVELS, ROWS, LANES),
            scratch(LEVELS, ROWS, LANES),
            scratch(tracers, LEVELS, ROWS, LANES),
            scratch(LEVELS, ROWS, LANES),
            scratch(LEVELS, ROWS, LANES),
            scratch(LEVELS // 2 + 1, tracers * ROWS, 2 * LANES),
            scratch(LEVELS // 2, tracers * ROWS, 2 * LANES),
        ],
    )
    args = (c_new, f_new, light, *heats)
    c_new, u_new, v_new, t_new, h_new = call(
        functools.partial(last_kernel, n),
        "last",
        args,
        [vmem] * len(args),
        [shape(*c.shape)] + [shape(*u.shape)] * FIELDS,
        out_specs=(anywhere,) * 5,
        scratch_shapes=[scratch(2, *u.shape), dma((FIELDS,)), dma((1,))],
    )
    return u_new, v_new, t_new, h_new, c_new


def solution(mesh):
    level = P("lon", ("grp", "lat", "role"), None)
    tracer = P(None, None, ("grp", "lat", "role"), "lon")
    return jax.shard_map(
        functools.partial(shards, mesh.shape["grp"], mesh.shape["lon"], mesh.shape["lat"]),
        mesh=mesh,
        in_specs=(level, level, level, level, tracer, P(("grp", "lat", "role"), None), P()),
        out_specs=(level, level, level, level, tracer),
        check_vma=False,
    )
```

```python
import functools

import jax
import jax.numpy as jnp
from jax import lax
from jax.experimental import pallas as pl
from jax.experimental.pallas import tpu as pltpu
from jax.sharding import PartitionSpec as P

ROWS = 8
LANES = 128
LEVELS = 8
CORES = 2
FIELDS = 4
NEAR = 3

RING_ROWS = 2 * ROWS
RING_COLS = 2 * LANES


def iota(shape, dim):
    return lax.broadcasted_iota(jnp.int32, shape, dim)


def roll(q, shift, axis):
    return pltpu.roll(q, shift % q.shape[axis], axis)


def position():
    lat, lon, role = lax.axis_index("lat"), lax.axis_index("lon"), lax.axis_index("role")
    return lat * CORES + role, lon, role


def block_of(m):
    return pl.ds(pl.multiple_of(m * LANES, LANES), LANES)


def packed(tracers, rates, tiles):
    lane = iota((ROWS, LANES), 1)
    zero = jnp.zeros((ROWS, LANES), jnp.float32)
    total, edge = [zero] * len(tiles), [zero] * len(tiles)
    for b in range(tracers):
        rate = rates[b]
        mine = lane // 4 == b
        for i, get in enumerate(tiles):
            q = get(b)
            total[i] = total[i] + rate * q
            edge[i] = jnp.where(mine, roll(q, 4 * b + 2, 1), edge[i])
    mine = lane // 4 == tracers
    return total, [jnp.where(mine, roll(t, 4 * tracers + 2, 1), e) for t, e in zip(total, edge)]


def last_rows(tiles):
    u, v, t, h = tiles
    sub = iota((ROWS, LANES), 0)
    low = jnp.where(sub >= 1, roll(t, -5, 0), roll(h, 1, 0))
    return jnp.where(sub >= 5, v, jnp.where(sub >= 3, roll(u, -3, 0), low))


def first_rows(tiles):
    u, v, t, h = tiles
    sub = iota((ROWS, LANES), 0)
    high = jnp.where(sub <= 6, roll(t, 5, 0), roll(h, -1, 0))
    return jnp.where(sub <= 2, v, jnp.where(sub <= 4, roll(u, 3, 0), high))


def next_rows(south, north, field):
    shift = (3, 0, 5, -1)[field]
    if shift:
        south, north = roll(south, shift, 0), roll(north, -shift, 0)
    return jnp.where(iota((ROWS, LANES), 0) >= ROWS // 2, south, north)


def sides_of(get, amount, east, west, into, start):
    lane = iota((ROWS, LANES), 1)
    for i in range(amount):
        first = start + 2 * NEAR * i
        side = jnp.where(lane < LANES // 2, get(i, east), get(i, west))
        into = jnp.where((lane >= first) & (lane < first + 2 * NEAR), roll(side, first + NEAR, 1), into)
    return into


def side_in(tile, i, start):
    return roll(tile, -(start + 2 * NEAR * i + NEAR), 1)


def load_kernel(n, u, v, t, h, count, rates, c, f_out, c_out, d_out, rates_out, z_out, r_out, sums, edges, first_rates, *refs):
    pays, (f_sem, c_sem) = refs[: n - 1], refs[n - 1 :]
    tracers, share = c.shape[0], f_out.shape[1]
    _, lon, role = position()
    upper = role == 1
    copies = [pltpu.make_async_copy(ref, f_out.at[i], f_sem.at[i]) for i, ref in enumerate((u, v, t, h))]
    copies.append(pltpu.make_async_copy(count, d_out, f_sem.at[FIELDS]))
    copies.append(pltpu.make_async_copy(rates, rates_out, f_sem.at[FIELDS + 1]))
    batch = tracers // c_sem.shape[0]
    c_copies = []
    for i in range(c_sem.shape[0]):
        part = pl.ds(i * batch, batch)
        c_copies.append(pltpu.make_async_copy(c.at[part], c_out.at[part], c_sem.at[i]))
    for copy in copies + c_copies:
        copy.start()
    for copy in copies:
        copy.wait()

    def whole(i, block):
        return f_out[i // share, i % share, :, block_of(block)]

    def strips_of(level, block):
        tiles = [whole(field * share + level, block) for field in range(FIELDS)]
        top, bottom = last_rows(tiles), first_rows(tiles)
        return jnp.where(upper, top, bottom), jnp.where(upper, bottom, top)

    count_f = FIELDS * share
    for level in range(share):
        for block in range(n):
            z_out[level * n + block], r_out[level * n + block] = strips_of(level, block)
    base = LEVELS
    for block in range(n):
        depth = d_out[:, block * LANES : (block + 1) * LANES].astype(jnp.float32)
        z_out[base + block] = depth
        r_out[base + block] = depth
    base += n
    for b in range(tracers):
        first_rates[b] = jnp.broadcast_to(rates_out[:1, b : b + 1], (ROWS, LANES))
    lane = iota((ROWS, LANES), 1)
    zero = jnp.zeros((ROWS, LANES), jnp.float32)
    total, edge = [zero] * LEVELS, [zero] * LEVELS
    for i, copy in enumerate(c_copies):
        copy.wait()
        for b in range(i * batch, (i + 1) * batch):
            for far in range(2):
                bottom, top = c_out[b, :, far, :], c_out[b, :, ROWS - 1 - far, :]
                z_out[base + 2 * b + far] = jnp.where(upper, top, bottom)
                r_out[base + 2 * b + far] = jnp.where(upper, bottom, top)
            for k in range(LEVELS):
                q = c_out[b, k]
                total[k] = total[k] + first_rates[b] * q
                edge[k] = jnp.where(lane // 4 == b, roll(q, 4 * b + 2, 1), edge[k])
    for k in range(LEVELS):
        edge[k] = jnp.where(lane // 4 == tracers, roll(total[k], 4 * tracers + 2, 1), edge[k])
        sums[k], edges[k] = total[k], edge[k]
    low = lane % 4 < 2
    for s, out in enumerate(pays):
        to_east = lax.rem(lon + (s + 1), n) > lon
        for i in range(LEVELS // 2):
            a, b = (jnp.where(to_east, q, roll(q, -2, 1)) for q in (edge[2 * i], edge[2 * i + 1]))
            out[i] = jnp.where(low, a, roll(b, 2, 1))


def join_kernel(n, rates, f, z, r, *refs):
    pays, x_outs, xz_outs = (refs[i * (n - 1) : (i + 1) * (n - 1)] for i in range(3))
    _, lon, _ = position()
    tracers, share, base = rates.shape[0], LEVELS // n, LEVELS + n
    _, (rim_r, rim_z) = packed(tracers, rates, [lambda b: r[base + 2 * b], lambda b: z[base + 2 * b]])
    zero = jnp.zeros((ROWS, LANES), jnp.float32)
    count = FIELDS * share

    def whole(i, block):
        return f[i // share, i % share, :, block_of(block)]

    for s, (pay, x, xz) in enumerate(zip(pays, x_outs, xz_outs)):
        m = lax.rem(lon + (s + 1), n)
        e, w = lax.rem(m + 1, n), lax.rem(m + n - 1, n)
        for i in range(count):
            x[i] = whole(i, m)
        x[count : count + LEVELS // 2] = pay[...]
        end = count + LEVELS // 2
        for level in range(share):
            x[end + level] = r[level * n + m]
            xz[level] = z[level * n + m]
        x[end + share] = rim_r
        sides = sides_of(whole, count, e, w, zero, 0)
        x[end + share + 1] = sides_of(
            lambda level, block: r[level * n + block], share, e, w, sides, 2 * NEAR * count
        )
        xz[share] = sides_of(lambda level, block: z[level * n + block], share, e, w, rim_z, 4 * (tracers + 1))


def split(q):
    high = q.astype(jnp.bfloat16)
    return high, (q - high.astype(jnp.float32)).astype(jnp.bfloat16)


def spread_kernel(rates, m_all, e_all):
    tracers = rates.shape[0]
    for group, transposed, size, out in ((ROWS, False, m_all.shape[0], m_all), (4, True, e_all.shape[1], e_all)):
        rows = (iota((size, tracers), 0) // group == iota((size, tracers), 1)).astype(jnp.bfloat16)
        cols = (iota((tracers, size), 1) // group == iota((tracers, size), 0)).astype(jnp.bfloat16)
        same = iota((size, size), 0) % group == iota((size, size), 1) % group
        parts = []
        for q in split(rates[...].T if transposed else rates[...]):
            wide = product(product(rows, q).astype(jnp.bfloat16), cols)
            parts.append(jnp.where(same, wide, 0.0).astype(jnp.bfloat16))
        high, low = parts
        out[...] = jnp.concatenate([high, high, low], axis=0 if transposed else 1)


def stacked(q, axis):
    high, low = split(q)
    return jnp.concatenate([high, low, high], axis=axis)


def product(left, right):
    return jnp.dot(left, right, preferred_element_type=jnp.float32)


def advected(q, e, w, up, down, stencil):
    a0, mu, pw, mv, ps = stencil
    return (a0 * q + (pw * w - mu * e)) + (ps * down - mv * up)


class Halo:
    def __init__(self, pos, strips):
        self.upper = pos[2] == 1
        end = jnp.logical_or(
            jnp.logical_and(pos[0] == 0, jnp.logical_not(self.upper)),
            jnp.logical_and(pos[0] == strips - 1, self.upper),
        )
        self.keep_z = jnp.where(end, 0.0, 1.0)
        self.from_r = (iota((ROWS, LANES), 0) >= ROWS // 2) == self.upper

    def rows(self, r, z):
        return jnp.where(self.from_r, r, z * self.keep_z)

    def sides(self, r, z):
        z = z * self.keep_z
        return jnp.where(self.upper, r, z), jnp.where(self.upper, z, r)


FIRST, SECOND = slice(0, LANES), slice(LANES, RING_COLS)
OWN_ROWS, FAR_ROWS = slice(0, ROWS), slice(ROWS, RING_ROWS)
WIDE = (RING_ROWS, RING_COLS)


def put(ref, at, tiles):
    places = ((OWN_ROWS, FIRST), (OWN_ROWS, SECOND), (FAR_ROWS, FIRST), (FAR_ROWS, SECOND))
    for tile, (rows, cols) in zip(tiles, places):
        ref[(*at, rows, cols)] = tile


def beside(m, n):
    return lax.rem(m + 1, n), lax.rem(m + n - 1, n)


def north(q):
    return roll(q, -1, 0)


def south(q):
    return roll(q, 1, 0)


def east(q):
    return roll(q, -1, 1)


def west(q):
    return roll(q, 1, 1)


def around(m, n):
    e, w = beside(m, n)
    ring_col = iota(WIDE, 1)
    block = jnp.where(ring_col < LANES, m, jnp.where(ring_col < LANES + LANES // 2, e, w))
    col = block * LANES + ring_col % LANES
    not_last, not_first = col < n * LANES - 1, col > 0
    return lambda q: jnp.where(not_last, east(q), 0.0), lambda q: jnp.where(not_first, west(q), 0.0)


def coriolis(strip, strips):
    ring_row = iota(WIDE, 0)
    row = strip * ROWS + jnp.where(ring_row < ROWS + ROWS // 2, ring_row, ring_row - RING_ROWS)
    return 0.3 * (2.0 * (row.astype(jnp.float32) + 0.5) / (strips * ROWS) - 1.0)


def masks(k, counts, east_of):
    wet = jnp.where(counts > k, 1.0, 0.0)
    return wet, wet * east_of(wet), wet * north(wet)


def advance(uu, vv, tt, wet_u, wet_v, turn, east_of, west_of, again):
    def mixed(q, e, w, nn):
        return 0.6 * q + 0.1 * ((e + w) + (nn + south(q)))

    te, tn = east_of(tt), north(tt)
    u_west = west(uu) if again else west_of(uu)
    u_new = wet_u * (mixed(uu, east(uu), u_west, north(uu)) + (turn * vv - 0.2 * (te - tt)))
    v_new = wet_v * (mixed(vv, east_of(vv), west_of(vv), north(vv)) - (turn * uu + 0.2 * (tn - tt)))
    return u_new, v_new, mixed(tt, te, west_of(tt), tn)


def coefficients(uu, vv):
    uu, vv = 0.5 * uu, 0.5 * vv
    uw, vs = west(uu), south(vv)
    pw, ps = jnp.maximum(uw, 0.0), jnp.maximum(vs, 0.0)
    mu, mv = jnp.minimum(uu, 0.0), jnp.minimum(vv, 0.0)
    a0 = (1.0 - (jnp.maximum(uu, 0.0) - jnp.minimum(uw, 0.0))) - (jnp.maximum(vv, 0.0) - jnp.minimum(vs, 0.0))
    return a0, mu, pw, mv, ps


def two_steps(read, wets, turn, shifts):
    uu, vv, tt = advance(read(0), read(1), read(2), *wets[1:], turn, *shifts, False)
    tt = wets[0] * (tt + 0.5 * read(3))
    stencil = coefficients(uu, vv)
    uu, vv, tt = advance(uu, vv, tt, *wets[1:], turn, *shifts, True)
    return uu, vv, wets[0] * tt, stencil, [q[OWN_ROWS, FIRST] for q in coefficients(uu, vv)]


def own_kernel(n, strips, rates, f, count, c, sums, z, r, coef1, coef2, wets, mix, f_out, dyn, depth):
    tracers, share = c.shape[0], f.shape[1]
    strip, lon, _ = pos = position()
    halo = Halo(pos, strips)
    lane = iota((ROWS, LANES), 1)
    base = LEVELS + n

    def window(main, near, m):
        e, w = beside(m, n)

        def side(g):
            return g(e) if n == 2 else jnp.where(lane < LANES // 2, g(e), g(w))

        return main(m), side(main), near(m), side(near)

    def own_window(field, level, m):
        def near(block):
            return next_rows(*halo.sides(r[level * n + block], z[level * n + block]), field)

        return window(lambda block: f[field, level, :, block_of(block)], near, m)

    def depth_window(m):
        return window(
            lambda block: count[:, block_of(block)].astype(jnp.float32),
            lambda block: halo.rows(r[LEVELS + block], z[LEVELS + block]),
            m,
        )

    put(depth, (), depth_window(lon))
    for field in range(FIELDS):
        for level in range(share):
            put(dyn, (field, level), own_window(field, level, lon))
    turn = coriolis(strip, strips)
    shifts = around(lon, n)
    for k in range(LEVELS):
        for i, q in enumerate(masks(float(k), depth[...], shifts[0])):
            wets[i, k] = q

    def one_level(level, carry):
        wet = [wets[i, lon * share + level] for i in range(3)]
        uu, vv, tt, stencil, stencil2 = two_steps(lambda i: dyn[i, level], wet, turn, shifts)
        for i, q in enumerate(stencil):
            coef1[i, lon * share + level] = q
        for i, q in enumerate(stencil2):
            coef2[i, lon * share + level] = q
        for i, q in enumerate((uu, vv, tt)):
            f_out[i, level, :, block_of(lon)] = q[OWN_ROWS, FIRST]
            if n == 2:
                f_out[i, level, :, block_of(1 - lon)] = q[OWN_ROWS, SECOND]
        return carry

    lax.fori_loop(0, share, one_level, 0, unroll=min(2, share))

    mix[0, :, OWN_ROWS] = c[0]
    mix[1, :, OWN_ROWS] = sums[...]
    for far in range(2):
        total = [jnp.zeros((LEVELS, LANES), jnp.float32)] * 2
        for b in range(tracers):
            rows = halo.sides(r[base + 2 * b + far], z[base + 2 * b + far])
            if b == 0:
                chl = rows
            total = [a + rates[b] * q for a, q in zip(total, rows)]
        for i, rows in enumerate((chl, total)):
            mix[i, :, RING_ROWS - 1 - far] = rows[0]
            mix[i, :, ROWS + far] = rows[1]

    if n > 2:

        def other_block(s, carry):
            m = lax.rem(lon + s, n)
            around_m = around(m, n)
            put(depth, (), depth_window(m))
            for level in range(share):
                k = (lon * share + level).astype(jnp.float32)
                for field in range(FIELDS):
                    put(dyn, (field, level), own_window(field, level, m))
                wet = masks(k, depth[...], around_m[0])
                after = two_steps(lambda i, level=level: dyn[i, level], wet, turn, around_m)
                for i, q in enumerate(after[:3]):
                    f_out[i, level, :, block_of(m)] = q[OWN_ROWS, FIRST]
            return carry

        lax.fori_loop(1, n, other_block, 0)


def flow_kernel(n, strips, tracers, *refs):
    wets, mix = refs[2:4]
    others = n - 1
    xs, xzs = (refs[6 + i * others : 6 + (i + 1) * others] for i in range(2))
    coef1, coef2, ends, rims, light_out = refs[6 + 2 * others : 11 + 2 * others]
    heats = refs[11 + 2 * others : 11 + 3 * others]
    dyn, side_mix, all_edges, all_rims, moved = refs[11 + 3 * others :]
    share = LEVELS // n
    strip, lon, _ = pos = position()
    halo = Halo(pos, strips)
    lane = iota((ROWS, LANES), 1)
    turn = coriolis(strip, strips)
    shifts = around(lon, n)

    fields = FIELDS * share
    end = fields + LEVELS // 2
    last_lane = 4 * (tracers + 1)
    for s, (x, xz) in enumerate(zip(xs, xzs)):
        m = lax.rem(lon + (n - 1 - s), n)
        sides, far_sides = x[end + share + 1], xz[share]
        for level in range(share):
            near = halo.sides(x[end + level], xz[level])
            corners = halo.sides(side_in(sides, level, 2 * NEAR * fields), side_in(far_sides, level, last_lane))
            for field in range(FIELDS):
                i = field * share + level
                put(
                    dyn,
                    (field, s * share + level),
                    (x[i], side_in(sides, i, 0), next_rows(*near, field), next_rows(*corners, field)),
                )
        all_edges[m] = x[fields:end]
        all_rims[m, 0], all_rims[m, 1] = halo.sides(x[end + share], far_sides)

    def other_level(i):
        s, level = i // share, i % share
        k = lax.rem(lon + (n - 1 - s), n) * share + level
        wet = [wets[j, k] for j in range(3)]
        _, _, _, stencil, stencil2 = two_steps(lambda j: dyn[j, i], wet, turn, shifts)
        for j, q in enumerate(stencil):
            coef1[j, k] = q
        for j, q in enumerate(stencil2):
            coef2[j, k] = q

    for i in range(others * share):
        other_level(i)

    east_m, west_m = beside(lon, n)
    easterly = lane % 4 >= 2
    exists = jnp.where(easterly, jnp.where(lon < n - 1, 1.0, 0.0), jnp.where(lon > 0, 1.0, 0.0))
    for k in range(LEVELS):
        e, w = all_edges[east_m, k // 2], all_edges[west_m, k // 2]
        if k % 2:
            w = roll(w, -2, 1)
        else:
            e = roll(e, 2, 1)
        ends[k] = jnp.where(easterly, e, w) * exists
    for side in range(2):
        rims[side] = jnp.where(easterly, all_rims[east_m, side], all_rims[west_m, side]) * exists

    for i, b in enumerate((0, tracers)):
        for k in range(LEVELS):
            side_mix[i, k, OWN_ROWS] = roll(ends[k], -(4 * b + 2), 1)
        for side, place in enumerate((RING_ROWS - 1, ROWS)):
            side_mix[i, :, place] = roll(rims[side], -(4 * b + 2), 1)

    levels = range(LEVELS)
    for k in levels:
        stencil = [coef1[i, k] for i in range(5)]
        for i in range(2):
            q = jnp.concatenate([mix[i, k], side_mix[i, k]], axis=1)
            moved[i, k] = advected(q, east(q), west(q), north(q), south(q), stencil)
    tau = jnp.zeros(WIDE, jnp.float32)
    top = tau + 1.0
    for k in levels:
        wet = wets[0, k]
        tau = tau + (0.1 + 0.3 * jnp.maximum(moved[0, k], 0.0))
        below = jnp.exp(-tau)
        light_out[0, k] = (wet * (top - below))[OWN_ROWS, FIRST]
        light = (0.5 * wet) * top
        coef1[5, k] = wet
        coef1[6, k] = light
        moved[0, k] = wet * moved[0, k] + light * moved[1, k]
        top = below
    inner = (OWN_ROWS, FIRST)
    tau = jnp.zeros((ROWS, LANES), jnp.float32)
    top = tau + 1.0
    for k in levels:
        chl = moved[0, k]
        stencil = [coef2[i, k] for i in range(5)]
        after = advected(*(q[inner] for q in (chl, east(chl), west(chl), north(chl), south(chl))), stencil)
        wet = wets[(0, k, *inner)]
        tau = tau + (0.1 + 0.3 * jnp.maximum(after, 0.0))
        below = jnp.exp(-tau)
        coef2[5, k] = wet
        coef2[6, k] = (0.5 * wet) * top
        light_out[1, k] = (2.0 * wet) * (top - below)
        top = below
    for s, heat in enumerate(heats):
        m = lax.rem(lon + (s + 1), n)
        for i in range(2):
            heat[i] = light_out[i, pl.ds(m * share, share)]


def tile_stencil(q, rim, columns, stencil, sub, lane):
    e = jnp.where(lane == LANES - 1, columns, roll(q, -1, 1))
    w = jnp.where(lane == 0, columns, roll(q, 1, 1))
    up = jnp.where(sub == ROWS - 1, rim, roll(q, -1, 0))
    down = jnp.where(sub == 0, rim, roll(q, 1, 0))
    return advected(q, e, w, up, down, stencil)


def swapped(q):
    return jnp.where(iota(q.shape, 1) % 4 == 1, roll(q, -1, 1), roll(q, 1, 1))


def beside_columns(edge, b):
    return roll(edge, LANES - 2 - 4 * b, 1)


def part_of(b, half):
    return slice(b * ROWS, (b + 1) * ROWS), slice(half * LANES, (half + 1) * LANES)


def tile_loop(pairs, source, rims, edge, coef, m_all, adv, store):
    tracers = source.shape[0]
    sub, lane = iota((ROWS, LANES), 0), iota((ROWS, LANES), 1)
    for i in pairs:
        for half in range(2):
            k = 2 * i + half
            stencil = [coef(j, k) for j in range(5)]
            columns = edge[k]
            for b in range(tracers):
                adv[(i, *part_of(b, half))] = tile_stencil(
                    source[b, k], rims[b, k], beside_columns(columns, b), stencil, sub, lane
                )
        react = product(m_all[...], stacked(adv[i], 0))
        for half in range(2):
            k = 2 * i + half
            wet, light = coef(5, k), coef(6, k)
            for b in range(tracers):
                store(b, k, wet * adv[(i, *part_of(b, half))] + light * react[part_of(b, half)])
        yield i


def tracer_kernel(
    n,
    strips,
    c,
    edges,
    ends,
    rims,
    coef,
    coef2,
    m_all,
    e_all,
    z,
    r,
    done,
    c_out,
    row1,
    edge1,
    row0,
    edge0,
    rim,
    adv,
    adv2,
):
    pos = position()
    tracers = c.shape[0]
    lon = pos[1]
    halo = Halo(pos, strips)
    sub, lane = iota((ROWS, LANES), 0), iota((ROWS, LANES), 1)
    easterly = lane % 4 >= 2
    base = LEVELS + n

    rim[:, 0, :] = rims[0]
    rim[:, ROWS - 1, :] = rims[1]
    parts = []
    for k in range(LEVELS):
        q, inside = ends[k], edges[k]
        outer = jnp.where(easterly, roll(q, -1, 1), roll(q, 1, 1))
        inner = jnp.where(easterly, roll(inside, 1, 1), roll(inside, -1, 1))
        up = jnp.where(sub == ROWS - 1, rim[k], roll(q, -1, 0))
        down = jnp.where(sub == 0, rim[k], roll(q, 1, 0))

        def at_edge(i):
            side = coef[i, k, :ROWS, LANES:]
            return (
                jnp.broadcast_to(side[:, :1], (ROWS, LANES)),
                jnp.broadcast_to(side[:, LANES - 1 :], (ROWS, LANES)),
            )

        def pick(pair):
            return jnp.where(easterly, pair[0], pair[1])

        stencil = [pick(at_edge(i)) for i in range(5)]
        wet, light = at_edge(5), at_edge(6)
        moved = advected(
            q, jnp.where(easterly, outer, inner), jnp.where(easterly, inner, outer), up, down, stencil
        )
        parts.append((moved, pick(wet), pick(light)))
        edge0[k] = swapped(q)
    react = product(stacked(jnp.concatenate([p[0] for p in parts], axis=0), 1), e_all[...])
    east_exists = jnp.where(lon < n - 1, 1.0, 0.0)
    west_exists = jnp.where(lon > 0, 1.0, 0.0)
    exists = jnp.where(easterly, east_exists, west_exists)
    for k, (q, wet, light) in enumerate(parts):
        edge1[k] = swapped((wet * q + light * react[k * ROWS : (k + 1) * ROWS]) * exists)

    places = ((0, RING_ROWS - 1), (ROWS - 1, ROWS))
    corners = [swapped(rims[side]) for side in range(2)]
    stencils = [[coef[i, :, place, :LANES] for i in range(7)] for _, place in places]
    for b in range(tracers):
        near = halo.sides(r[base + 2 * b], z[base + 2 * b])
        far = halo.sides(r[base + 2 * b + 1], z[base + 2 * b + 1])
        for side, (at, _) in enumerate(places):
            q = near[side]
            row0[b, :, at, :] = q
            columns = beside_columns(corners[side], b)
            e = jnp.where(lane == LANES - 1, columns, roll(q, -1, 1))
            w = jnp.where(lane == 0, columns, roll(q, 1, 1))
            inner = c[b, :, at, :]
            up, down = (inner, far[side]) if side == 0 else (far[side], inner)
            adv[(LEVELS // 2, *part_of(b, side))] = advected(q, e, w, up, down, stencils[side][:5])
    react = product(m_all[...], stacked(adv[LEVELS // 2], 0))
    for b in range(tracers):
        for side, (at, _) in enumerate(places):
            wet, light = stencils[side][5:]
            row1[b, :, at, :] = wet * adv[(LEVELS // 2, *part_of(b, side))] + light * react[part_of(b, side)]

    def store(b, k, q):
        c_out[b, k] = q

    def store_done(b, k, q):
        done[b, k] = q

    pairs = range(LEVELS // 2)
    for _ in tile_loop(pairs, c, row0, edge0, lambda i, k: coef[i, k, :ROWS, :LANES], m_all, adv, store):
        pass
    for _ in tile_loop(pairs, c_out, row1, edge1, lambda i, k: coef2[i, k], m_all, adv2, store_done):
        pass


def last_kernel(n, *refs):
    others = n - 1
    c, f, light, heats = *refs[:3], refs[3 : 3 + others]
    c_out, u_out, v_out, t_out, h_out, warm, sem, c_sem = refs[3 + others :]
    copies = [pltpu.make_async_copy(f.at[i], ref, sem.at[i]) for i, ref in enumerate((u_out, v_out))]
    batch = c.shape[0] // c_sem.shape[0]
    for i in range(c_sem.shape[0]):
        part = pl.ds(i * batch, batch)
        copies.append(pltpu.make_async_copy(c.at[part], c_out.at[part], c_sem.at[i]))
    for copy in copies:
        copy.start()
    share = f.shape[1]
    _, lon, _ = position()
    here = block_of(lon)
    for level in range(share):
        k = lon * share + level
        warm[0, level, :, here] = f[2, level, :, here] + light[0, k]
        warm[1, level, :, here] = light[1, k]
        for s, heat in enumerate(heats):
            there = block_of(lax.rem(lon + (n - 1 - s), n))
            warm[0, level, :, there] = f[2, level, :, there] + heat[0, level]
            warm[1, level, :, there] = heat[1, level]
    copies += [pltpu.make_async_copy(warm.at[i], ref, sem.at[2 + i]) for i, ref in enumerate((t_out, h_out))]
    for copy in copies[-2:]:
        copy.start()
    for copy in copies:
        copy.wait()


def shards(groups, n, lats, u, v, t, h, c, count, rates):
    tracers = c.shape[0]
    share, width = u.shape[0], u.shape[2]
    strips = lats * CORES
    vmem = pl.BlockSpec(memory_space=pltpu.VMEM)
    anywhere = pl.BlockSpec(memory_space=pl.ANY)
    hbm = pl.BlockSpec(memory_space=pltpu.HBM)
    params = pltpu.CompilerParams(vmem_limit_bytes=32 * 1024 * 1024)
    dma = pltpu.SemaphoreType.DMA

    def shape(*dims, dtype=jnp.float32):
        return jax.ShapeDtypeStruct(dims, dtype)

    def tiles(*dims):
        return shape(*dims, ROWS, LANES)

    def scratch(*dims):
        return pltpu.VMEM(dims, jnp.float32)

    def call(kernel, name, args, in_specs, out_shape, out_specs=None, **options):
        return pl.pallas_call(
            kernel,
            out_shape=tuple(out_shape),
            in_specs=in_specs,
            out_specs=out_specs or (vmem,) * len(out_shape),
            **options,
            compiler_params=params,
            name=name,
        )(*args)

    def permute(q, target):
        pairs = []
        for g in range(groups):
            for a in range(lats):
                for o in range(n):
                    for i in range(CORES):
                        g2, a2, o2, i2 = target(g, a, o, i)
                        pairs.append(
                            (((g * lats + a) * n + o) * CORES + i, ((g2 * lats + a2) * n + o2) * CORES + i2)
                        )
        return lax.ppermute(q, ("grp", "lat", "lon", "role"), pairs)

    def z_target(shift):
        def target(g, a, o, i):
            s = a * CORES + i + (1 if i else -1)
            if 0 <= s < strips:
                return g, s // CORES, (o + shift) % n, s % CORES
            return (g ^ 1 if g ^ 1 < groups else g), a, o, i

        return target

    def x_target(shift):
        return lambda g, a, o, i: (g, a, (o + shift) % n, i)

    def r_target(g, a, o, i):
        return g, a, o, 1 - i

    shifts = range(1, n)
    z_tiles = LEVELS + n + 2 * tracers
    f, c_here, depth, rates, z_pay, r_pay, sums, edges, first_rates, *pays = call(
        functools.partial(load_kernel, n),
        "load",
        [pltpu.with_memory_space_constraint(q, pltpu.HBM) for q in (u, v, t, h, count, rates, c)],
        [hbm] * 7,
        [
            shape(FIELDS, *u.shape),
            shape(*c.shape),
            shape(*count.shape, dtype=jnp.int32),
            shape(*rates.shape),
            tiles(z_tiles),
            tiles(z_tiles),
            tiles(LEVELS),
            tiles(LEVELS),
            tiles(tracers),
        ]
        + [tiles(LEVELS // 2)] * (n - 1),
        scratch_shapes=[dma((FIELDS + 2,)), dma((2,))],
    )
    r_in = permute(r_pay, r_target)
    z_in = permute(z_pay, z_target(0))
    pays = call(
        functools.partial(join_kernel, n),
        "join",
        (first_rates, f, z_pay, r_in, *pays),
        [vmem] * (n + 3),
        [tiles(FIELDS * share + LEVELS // 2 + share + 2)] * (n - 1) + [tiles(share + 1)] * (n - 1),
    )
    xs = [permute(q, x_target(s)) for s, q in zip(shifts, pays[: n - 1])]
    xzs = [permute(q, z_target(s)) for s, q in zip(shifts, pays[n - 1 :])]

    m_size, e_size = tracers * ROWS, LANES
    bf16 = jnp.bfloat16
    m_all, e_all = call(
        spread_kernel,
        "spread",
        (rates,),
        [vmem],
        [shape(m_size, 3 * m_size, dtype=bf16), shape(3 * e_size, e_size, dtype=bf16)],
    )

    args = (first_rates, f, depth, c_here, sums, z_in, r_in)
    own1, own2, wets, mix, f_new = call(
        functools.partial(own_kernel, n, strips),
        "own",
        args,
        [vmem] * len(args),
        [
            shape(7, LEVELS, RING_ROWS, RING_COLS),
            tiles(7, LEVELS),
            shape(3, LEVELS, RING_ROWS, RING_COLS),
            shape(2, LEVELS, RING_ROWS, LANES),
            shape(3, *u.shape),
        ],
        scratch_shapes=[scratch(FIELDS, share, RING_ROWS, RING_COLS), scratch(RING_ROWS, RING_COLS)],
    )
    args = (own1, own2, wets, mix, m_all, e_all, *xs, *xzs)
    coef1, coef2, ends, rims, light, *heats = call(
        functools.partial(flow_kernel, n, strips, tracers),
        "flow",
        args,
        [vmem] * len(args),
        [
            shape(7, LEVELS, RING_ROWS, RING_COLS),
            tiles(7, LEVELS),
            tiles(LEVELS),
            shape(2, LEVELS, LANES),
            tiles(2, LEVELS),
        ]
        + [tiles(2, share)] * (n - 1),
        input_output_aliases={0: 0, 1: 1},
        scratch_shapes=[
            scratch(FIELDS, (n - 1) * share, RING_ROWS, RING_COLS),
            scratch(2, LEVELS, RING_ROWS, LANES),
            scratch(n, LEVELS // 2, ROWS, LANES),
            scratch(n, 2, LEVELS, LANES),
            scratch(2, LEVELS, RING_ROWS, RING_COLS),
        ],
    )
    heats = [permute(q, x_target(s)) for s, q in zip(shifts, heats)]
    args = (c_here, edges, ends, rims, coef1, coef2, m_all, e_all, z_in, r_in)
    (c_new,) = call(
        functools.partial(tracer_kernel, n, strips),
        "tracers",
        args,
        [vmem] * len(args),
        [shape(*c.shape)],
        scratch_shapes=[
            scratch(*c.shape),
            scratch(tracers, LEVELS, ROWS, LANES),
            scratch(LEVELS, ROWS, LANES),
            scratch(tracers, LEVELS, ROWS, LANES),
            scratch(LEVELS, ROWS, LANES),
            scratch(LEVELS, ROWS, LANES),
            scratch(LEVELS // 2 + 1, tracers * ROWS, 2 * LANES),
            scratch(LEVELS // 2, tracers * ROWS, 2 * LANES),
        ],
    )
    args = (c_new, f_new, light, *heats)
    c_new, u_new, v_new, t_new, h_new = call(
        functools.partial(last_kernel, n),
        "last",
        args,
        [vmem] * len(args),
        [shape(*c.shape)] + [shape(*u.shape)] * FIELDS,
        out_specs=(anywhere,) * 5,
        scratch_shapes=[scratch(2, *u.shape), dma((FIELDS,)), dma((1,))],
    )
    return u_new, v_new, t_new, h_new, c_new


def solution(mesh):
    level = P("lon", ("grp", "lat", "role"), None)
    tracer = P(None, None, ("grp", "lat", "role"), "lon")
    return jax.shard_map(
        functools.partial(shards, mesh.shape["grp"], mesh.shape["lon"], mesh.shape["lat"]),
        mesh=mesh,
        in_specs=(level, level, level, level, tracer, P(("grp", "lat", "role"), None), P()),
        out_specs=(level, level, level, level, tracer),
        check_vma=False,
    )
```
